32 devices in a mesh: seq: 2 (over x), row: 4 (over y, core), col: 4 (over z).
Axes of the slice: x: 2, y: 2, z: 4, core: 2. Of those that a mesh axis runs over, the one named last changes fastest.
Arguments:
- inputs: bfloat16 [4, 16, 64, 4096], P('row', 'seq', None, 'col'), may hold values from -8 to 8
- query_proj: bfloat16 [4, 16, 64, 4096], P('row', 'seq', None, 'col'), may hold values from -5 to 5
- key_proj: bfloat16 [4, 16, 64, 4096], P('row', 'seq', None, 'col'), may hold values from -5 to 5
- value_proj: bfloat16 [4, 16, 64, 4096], P('row', 'seq', None, 'col'), may hold values from -6 to 6
- depth_weight: bfloat16 [7, 7, 4096], P(None, None, 'col'), may hold values from -1.25 to 1.25
- depth_bias: bfloat16 [4096], P('col'), may hold values from -3 to 3
- norm_gain: bfloat16 [4096], replicated, may hold values from 0.099609375 to 1.8984375
- norm_bias: bfloat16 [4096], replicated, may hold values from -3 to 3
- expand_weight: bfloat16 [4096, 16384], P(('seq', 'row'), 'col'), may hold values from -0.09375 to 0.09375
- expand_bias: bfloat16 [16384], P('col'), may hold values from -3 to 3
Outputs:
- residual_out: bfloat16 [4, 16, 64, 4096], P('row', 'seq', None, 'col')
- hidden: bfloat16 [4, 16, 64, 16384], P('row', 'seq', None, 'col')
The draws below stay inside these ranges and needn't reach their ends.
All inputs are finite; a program needn't handle non-finite values.
Results may differ from the reference program's by a relative error of at most 0.0075.
Values may be sent and summed in bfloat16 or wider, within the bound.
A program may use at most 128 MiB of HBM per device.

```python
import math
import jax
import jax.numpy as jnp
from jax import lax

C = 4096
FF = 16384
HEAD_DIM = 128
KERNEL = 7
IMG_W = 64
HEADS = 32
IMG_H = 16
BATCH = 4


def draw_inputs(key, part):
    scale_key = jax.random.fold_in(key, 21)
    value_key = jax.random.fold_in(key, 22)
    row_scale = jnp.exp(jax.random.uniform(scale_key, (BATCH, IMG_H, IMG_W, 1), jnp.float32, math.log(0.3), math.log(3.0)))
    values = row_scale * jax.random.normal(value_key, (BATCH, IMG_H, IMG_W, C), jnp.float32)
    return jnp.clip(values, -8.0, 8.0).astype(jnp.bfloat16)


def base_draw(key, marker):
    sub_key = jax.random.fold_in(key, marker)
    shaped = (BATCH, IMG_H * IMG_W, HEADS, HEAD_DIM)
    values = jnp.clip(1.41 * jax.random.normal(sub_key, shaped, jnp.float32), -5.0, 5.0)
    return values


def draw_query_proj(key, part):
    values = base_draw(key, 41)
    return values.reshape(BATCH, IMG_H, IMG_W, C).astype(jnp.bfloat16)


def draw_key_proj(key, part):
    values = base_draw(key, 42)
    return values.reshape(BATCH, IMG_H, IMG_W, C).astype(jnp.bfloat16)


def draw_depth_weight(key, part):
    scale_key = jax.random.fold_in(key, 51)
    value_key = jax.random.fold_in(key, 52)
    channel_scale = jnp.exp(jax.random.uniform(scale_key, (1, 1, C), jnp.float32, math.log(0.3), math.log(3.0)))
    values = jax.random.normal(value_key, (KERNEL, KERNEL, C), jnp.float32)
    return jnp.clip(values * channel_scale / KERNEL, -1.25, 1.25).astype(jnp.bfloat16)


def block_levels(own_key, extent, pieces, least, largest):
    level = 1.0
    for position, blocks in pieces:
        heights = jax.random.uniform(jax.random.fold_in(jax.random.fold_in(own_key, 6), position), (blocks,), jnp.float32, least / len(pieces), largest / len(pieces))
        level = level * jnp.repeat(jnp.exp(heights), extent[position] // blocks).reshape((-1,) + (1,) * (len(extent) - 1 - position))
    return level


def centred(rng, shape, scale, most, pieces=(), kind=jnp.bfloat16):
    array = scale * jax.random.normal(rng, shape, jnp.float32)
    if pieces:
        array = array * block_levels(rng, shape, pieces, -0.22, 0.18)
    return jnp.clip(array, -most, most).astype(kind)


def setup_inputs(seed: int = 0) -> dict:
    streams_of = jax.random.split(jax.random.key(seed), 11)
    inputs = draw_inputs(jax.random.fold_in(streams_of[10], 71), 0)
    query_proj = draw_query_proj(jax.random.fold_in(streams_of[10], 71), 0)
    key_proj = draw_key_proj(jax.random.fold_in(streams_of[10], 71), 0)
    value_proj = centred(streams_of[3], (BATCH, IMG_H, IMG_W, C), 1.0, 6.0, ((0, 4), (1, 2), (3, 4)))
    depth_weight = draw_depth_weight(jax.random.fold_in(streams_of[10], 71), 0)
    depth_bias = centred(streams_of[5], (C,), 0.5, 3.0, ((0, 4),))
    norm_gain = jnp.clip(1.0 + 0.18 * jax.random.normal(streams_of[6], (C,), jnp.float32), 0.099609375, 1.8984375).astype(jnp.bfloat16)
    norm_bias = centred(streams_of[7], (C,), 0.5, 3.0)
    expand_weight = centred(streams_of[8], (C, FF), C ** -0.5, 0.09375, ((0, 8), (1, 4)))
    expand_bias = centred(streams_of[9], (FF,), 0.5, 3.0, ((0, 4),))
    return dict(inputs=inputs, query_proj=query_proj, key_proj=key_proj, value_proj=value_proj, depth_weight=depth_weight, depth_bias=depth_bias, norm_gain=norm_gain, norm_bias=norm_bias, expand_weight=expand_weight, expand_bias=expand_bias)


def settle(values):
    return lax.optimization_barrier(values.astype(jnp.bfloat16))

def attend_sample(parts):
    queries, keys_in, values_in = parts
    scores = jnp.einsum('qhd,khd->hqk', queries.astype(jnp.float32), keys_in.astype(jnp.float32)) * (1.0 / math.sqrt(HEAD_DIM))
    peak = lax.optimization_barrier(jnp.max(scores, axis=-1, keepdims=True))
    weights = jnp.exp(scores - peak)
    total = lax.optimization_barrier(jnp.sum(weights, axis=-1))
    rounded = settle(weights).astype(jnp.float32)
    summed = jnp.einsum('hqk,khd->qhd', rounded, values_in.astype(jnp.float32))
    return summed / jnp.transpose(total)[:, :, None]

def reference(inputs, query_proj, key_proj, value_proj, depth_weight, depth_bias, norm_gain, norm_bias, expand_weight, expand_bias):
    positions = IMG_H * IMG_W
    shaped = (BATCH, positions, HEADS, HEAD_DIM)
    attended = lax.map(attend_sample, (query_proj.reshape(shaped), key_proj.reshape(shaped), value_proj.reshape(shaped)))
    attended = attended.reshape(BATCH, IMG_H, IMG_W, C)
    residual_out = (inputs.astype(jnp.float32) + attended).astype(jnp.bfloat16)
    margin = KERNEL // 2
    padded = jnp.pad(settle(residual_out).astype(jnp.float32), ((0, 0), (margin, margin), (margin, margin), (0, 0)))
    kernel_taps = depth_weight.astype(jnp.float32)
    convolved = jnp.zeros((BATCH, IMG_H, IMG_W, C), jnp.float32)
    for row_tap in range(KERNEL):
        for col_tap in range(KERNEL):
            convolved = convolved + padded[:, row_tap:row_tap + IMG_H, col_tap:col_tap + IMG_W, :] * kernel_taps[row_tap, col_tap]
    convolved = settle(convolved + depth_bias.astype(jnp.float32))
    widened = convolved.reshape(BATCH * positions, C).astype(jnp.float32)
    center = lax.optimization_barrier(jnp.mean(widened, axis=1, keepdims=True))
    spread = lax.optimization_barrier(jnp.mean((widened - center) * (widened - center), axis=1, keepdims=True))
    normed = ((widened - center) / jnp.sqrt(spread + 1e-06) * norm_gain.astype(jnp.float32) + norm_bias.astype(jnp.float32)).astype(jnp.bfloat16)
    project = jnp.dot(normed, expand_weight, preferred_element_type=jnp.float32)
    hidden = jax.nn.gelu(project + expand_bias.astype(jnp.float32), approximate=False).astype(jnp.bfloat16)
    return (residual_out, hidden.reshape(BATCH, IMG_H, IMG_W, FF))
```

```python
import functools
import math

import jax
import jax.numpy as jnp
from jax import lax
from jax.experimental import pallas as pl
from jax.experimental.pallas import tpu as pltpu
from jax.sharding import PartitionSpec as P

HEAD_DIM = 128
KERNEL = 7
VMEM_BYTES = 62 * 1024 * 1024


def padded_2(array, sides, width):
    for axis, dim in sides:
        peers, length = (lax.axis_size(axis), array.shape[dim])
        up = [(i, (i + 1) % peers) for i in range(peers - 1)]
        down = [(j, i) for i, j in up]
        last = lax.slice_in_dim(array, length - width, length, axis=dim)
        leading = lax.slice_in_dim(array, 0, width, axis=dim)
        before = lax.ppermute(last, axis, up)
        after = lax.ppermute(leading, axis, down)
        array = jnp.concatenate([before, array, after], axis=dim)
    return array


def on_device(
    inputs,
    query_proj,
    key_proj,
    value_proj,
    depth_weight,
    depth_bias,
    norm_gain,
    norm_bias,
    expand_weight,
    expand_bias,
):
    samples, rows_here, col_count, channels = inputs.shape
    heads_here = channels // HEAD_DIM
    positions = rows_here * col_count
    score_scale = 1.0 / math.sqrt(HEAD_DIM)
    queries = query_proj.reshape(samples, positions, heads_here, HEAD_DIM)
    start_max = jnp.full((samples, heads_here, positions), -1e30, jnp.float32)
    keys_in = lax.all_gather(key_proj, "seq", axis=1, tiled=True)
    values_in = lax.all_gather(value_proj, "seq", axis=1, tiled=True)
    count = keys_in.shape[1] * keys_in.shape[2]
    keys_in = keys_in.reshape(samples, count, heads_here, HEAD_DIM)
    values_in = values_in.reshape(samples, count, heads_here, HEAD_DIM)
    scores = (
        jnp.einsum("bqhd,bkhd->bhqk", queries, keys_in, preferred_element_type=jnp.float32)
        * score_scale
    )
    new_max = jnp.maximum(start_max, jnp.max(scores, axis=-1))
    weights = jnp.exp(scores - new_max[..., None])
    new_total = jnp.sum(weights, axis=-1)
    update = jnp.einsum(
        "bhqk,bkhd->bhqd",
        weights.astype(jnp.bfloat16),
        values_in,
        preferred_element_type=jnp.float32,
    )
    attended = update / new_total[..., None]
    attended = jnp.transpose(attended, (0, 2, 1, 3)).reshape(
        samples, rows_here, col_count, channels
    )
    residual_out = (inputs.astype(jnp.float32) + attended).astype(jnp.bfloat16)
    margin = KERNEL // 2
    padded = padded_2(residual_out, (("seq", 1),), margin)
    padded = jnp.pad(padded, ((0, 0), (0, 0), (margin, margin), (0, 0))).astype(jnp.float32)
    kernel_taps = depth_weight.astype(jnp.float32)
    convolved = jnp.zeros((samples, rows_here, col_count, channels), jnp.float32)
    for row_tap in range(KERNEL):
        for col_tap in range(KERNEL):
            convolved = (
                convolved
                + padded[:, row_tap : row_tap + rows_here, col_tap : col_tap + col_count, :]
                * kernel_taps[row_tap, col_tap]
            )
    convolved = (convolved + depth_bias.astype(jnp.float32)).astype(jnp.bfloat16)
    flat_rows = convolved.reshape(samples * positions, channels)
    gathered = lax.all_gather(flat_rows, "col", axis=1, tiled=True)
    widened = gathered.astype(jnp.float32)
    center = jnp.mean(widened, axis=1, keepdims=True)
    spread = jnp.mean((widened - center) * (widened - center), axis=1, keepdims=True)
    normed = (
        (widened - center) * lax.rsqrt(spread + 1e-06) * norm_gain.astype(jnp.float32)
        + norm_bias.astype(jnp.float32)
    ).astype(jnp.bfloat16)
    project = jnp.dot(
        normed,
        lax.all_gather(expand_weight, ("seq", "row"), axis=0, tiled=True),
        preferred_element_type=jnp.float32,
    )
    hidden = jax.nn.gelu(project + expand_bias.astype(jnp.float32), approximate=False).astype(
        jnp.bfloat16
    )
    return (residual_out, hidden.reshape(samples, rows_here, col_count, expand_weight.shape[1]))


def whole_block(
    x_ref, q_ref, k_ref, v_ref, taps_ref, dbias_ref, gain_ref, nbias_ref, w_ref, ebias_ref,
    res_ref, out_ref,
    k_in, v_in, halo, rows_f32, shifted, acts, weights, total,
    kv_send, kv_recv, halo_send, halo_recv, z_send, z_recv, own_sem,
    y_send, y_recv, x_send, x_recv, far_send, far_recv, core_send, core_recv,
    *, heads, rows, width, planes,
):
    seq, row, col = (lax.axis_index(a) for a in ("seq", "row", "col"))
    positions = rows * width
    margin = KERNEL // 2
    strip = margin * width
    chans = heads * HEAD_DIM
    depth = w_ref.shape[0]
    pieces, piece = total.shape[0], total.shape[2]
    to_x = {"seq": 1 - seq}
    to_y = {"row": lax.rem(row + 2, 4)}
    to_core = {"row": row + 1 - 2 * lax.rem(row, 2)}
    z_peers = [{"col": lax.rem(col + i, planes)} for i in range(1, planes)]

    def remote(src, dst, send, recv, where):
        return pltpu.make_async_remote_copy(
            src_ref=src, dst_ref=dst, send_sem=send, recv_sem=recv,
            device_id=where, device_id_type=pl.DeviceIdType.MESH,
        )

    def lanes(h):
        return pl.ds(pl.multiple_of(h * HEAD_DIM, HEAD_DIM), HEAD_DIM)

    def key_copy(h):
        return remote(k_ref.at[:, lanes(h)], k_in.at[h], kv_send.at[h], kv_recv.at[h], to_x)

    def value_copy(h):
        return remote(
            v_ref.at[:, lanes(h)], v_in.at[h], kv_send.at[heads + h], kv_recv.at[heads + h], to_x
        )

    def halo_copy(h):
        start = pl.multiple_of((1 - seq) * (positions - strip), width)
        return remote(
            res_ref.at[pl.ds(start, strip), lanes(h)], halo.at[h],
            halo_send.at[h], halo_recv.at[h], to_x,
        )

    def act_lanes(h, plane):
        return pl.ds(pl.multiple_of(plane * chans + h * HEAD_DIM, HEAD_DIM), HEAD_DIM)

    def act_copy(h, i):
        part = acts.at[:, act_lanes(h, col)]
        return remote(
            part, part, z_send.at[i * heads + h], z_recv.at[i * heads + h], z_peers[i]
        )

    def act_arrival(h, i):
        plane = lax.rem(col + planes - i - 1, planes)
        part = acts.at[:, act_lanes(h, plane)]
        return remote(
            part, part, z_send.at[i * heads + h], z_recv.at[i * heads + h], z_peers[i]
        )

    def own_piece(j):
        return w_ref.at[:, pl.ds(j * piece, piece)]

    def own_copy(j):
        return pltpu.make_async_copy(own_piece(j), weights.at[0, j], own_sem.at[j])

    def y_copy(j):
        return remote(own_piece(j), weights.at[1, j], y_send.at[j], y_recv.at[j], to_y)

    def x_copy(j):
        return remote(own_piece(j), weights.at[2, j], x_send.at[j], x_recv.at[j], to_x)

    def far_copy(j):
        if j < pieces - 1:
            return remote(
                weights.at[2, j], weights.at[3, j], far_send.at[j], far_recv.at[j], to_y
            )
        return remote(weights.at[1, j], weights.at[3, j], far_send.at[j], far_recv.at[j], to_x)

    def core_copy(b, j):
        src = own_piece(j) if b == 0 else weights.at[b, j]
        at = b * pieces + j
        return remote(src, weights.at[4 + b, j], core_send.at[at], core_recv.at[at], to_core)

    barrier = pltpu.get_barrier_semaphore()
    peers = [to_x, to_y, to_core] + z_peers
    for peer in peers:
        pl.semaphore_signal(
            barrier, inc=1, device_id=peer, device_id_type=pl.DeviceIdType.MESH
        )
    pl.semaphore_wait(barrier, len(peers))

    @pl.loop(0, heads)
    def _(h):
        key_copy(h).start()
        value_copy(h).start()

    for j in range(pieces):
        y_copy(j).start()
    for j in range(pieces):
        own_copy(j).start()
        core_copy(0, j).start()

    scale = 1.0 / math.sqrt(HEAD_DIM)
    half = positions // 2
    shifted[...] = jnp.zeros_like(shifted)

    def attend(h):
        keys, values = k_ref[:, lanes(h)], v_ref[:, lanes(h)]
        far_keys, far_values = k_in[h], v_in[h]
        over = (((1,), (1,)), ((), ()))

        @pl.loop(0, 2)
        def _(i):
            here = pl.ds(pl.multiple_of(i * half, half), half)
            queries = q_ref[here, lanes(h)]
            near = lax.dot_general(queries, keys, over, preferred_element_type=jnp.float32) * scale
            far = lax.dot_general(queries, far_keys, over, preferred_element_type=jnp.float32) * scale
            peak = jnp.maximum(
                jnp.max(near, axis=1, keepdims=True), jnp.max(far, axis=1, keepdims=True)
            )
            near, far = jnp.exp(near - peak), jnp.exp(far - peak)
            count = jnp.sum(near, axis=1, keepdims=True) + jnp.sum(far, axis=1, keepdims=True)
            mixed = jnp.dot(
                near.astype(jnp.bfloat16), values, preferred_element_type=jnp.float32
            ) + jnp.dot(far.astype(jnp.bfloat16), far_values, preferred_element_type=jnp.float32)
            res_ref[here, lanes(h)] = (
                x_ref[here, lanes(h)].astype(jnp.float32) + mixed / count
            ).astype(jnp.bfloat16)

    def convolve(h):
        edge = halo[h].astype(jnp.float32)
        lead, trail = margin * width, (margin + rows) * width
        rows_f32[0:lead, :] = jnp.where(seq == 1, edge, 0.0)
        rows_f32[lead:trail, :] = res_ref[:, lanes(h)].astype(jnp.float32)
        rows_f32[trail:, :] = jnp.where(seq == 0, edge, 0.0)
        group = 4

        @pl.loop(0, rows // group)
        def _(g):
            base = g * (group * width)
            for q in range(KERNEL):
                sums = [None] * group
                for r in range(group + KERNEL - 1):
                    start = pl.multiple_of(base + r * width, width)
                    line = rows_f32[pl.ds(start, width), :]
                    for o in range(group):
                        p = r - o
                        if 0 <= p < KERNEL:
                            term = line * taps_ref[pl.ds(p * KERNEL + q, 1), lanes(h)]
                            sums[o] = term if sums[o] is None else sums[o] + term
                for o in range(group):
                    shifted[o, q, 8 : 8 + width, :] = sums[o]
            for o in range(group):
                value = shifted[o, margin, 8 : 8 + width, :] + dbias_ref[:, lanes(h)]
                for q in range(KERNEL):
                    if q != margin:
                        begin = 8 + q - margin
                        value = value + shifted[o, q, begin : begin + width, :]
                start = pl.multiple_of(base + o * width, width)
                acts[pl.ds(start, width), act_lanes(h, col)] = value.astype(jnp.bfloat16)

    @pl.loop(0, heads + 1)
    def _(h):
        @pl.when(h < heads)
        def _():
            key_copy(h).wait_recv()
            value_copy(h).wait_recv()

            @pl.when(h == heads - 1)
            def _():
                x_copy(0).start()

            attend(h)
            halo_copy(h).start()

        @pl.when(h == heads)
        def _():
            for j in range(1, pieces):
                x_copy(j).start()

        @pl.when(h > 0)
        def _():
            halo_copy(h - 1).wait_recv()
            convolve(h - 1)
            for i in range(planes - 1):
                act_copy(h - 1, i).start()

    def y_arrived(j):
        y_copy(j).wait_recv()
        core_copy(1, j).start()
        if j == pieces - 1:
            far_copy(j).start()

    def x_arrived(j):
        x_copy(j).wait_recv()
        if j < pieces - 1:
            far_copy(j).start()
        core_copy(2, j).start()

    def far_arrived(j):
        far_copy(j).wait_recv()
        core_copy(3, j).start()

    y_arrived(0)
    y_arrived(1)
    x_arrived(0)
    y_arrived(2)
    x_arrived(1)
    y_arrived(3)

    @pl.loop(0, heads)
    def _(h):
        for i in range(planes - 1):
            act_arrival(h, i).wait_recv()
            act_copy(h, i).wait_send()

    x_arrived(2)
    block = 16
    inverse = 1.0 / acts.shape[1]

    @pl.loop(0, positions // block)
    def _(i):
        here = pl.ds(pl.multiple_of(i * block, block), block)
        wide = acts[here, :].astype(jnp.float32)
        center = jnp.sum(wide, axis=1, keepdims=True) * inverse
        wide = wide - center
        spread = jnp.sum(wide * wide, axis=1, keepdims=True) * inverse
        acts[here, :] = (
            wide * lax.rsqrt(spread + 1e-06) * gain_ref[...] + nbias_ref[...]
        ).astype(jnp.bfloat16)

    other = row + 1 - 2 * lax.rem(row, 2)
    places = []
    for r in (row, other):
        y = lax.rem(r + 2, 4)
        places.append([seq * 4 + r, seq * 4 + y, (1 - seq) * 4 + r, (1 - seq) * 4 + y])
    places = places[0] + places[1]

    def product(here, j, slots):
        result = None
        for slot in slots:
            cols = pl.ds(pl.multiple_of(places[slot] * depth, depth), depth)
            term = jnp.dot(
                acts[here, cols], weights[slot, j], preferred_element_type=jnp.float32
            )
            result = term if result is None else result + term
        return result

    tile = 256

    def first(j):
        @pl.loop(0, positions // tile)
        def _(i):
            here = pl.ds(pl.multiple_of(i * tile, tile), tile)
            total[j, here, :] = product(here, j, (0, 4, 1, 5))

    def second(j):
        core_copy(2, j).wait_recv()

        @pl.loop(0, positions // tile)
        def _(i):
            here = pl.ds(pl.multiple_of(i * tile, tile), tile)
            total[j, here, :] += product(here, j, (2, 6))

    def third(j):
        core_copy(3, j).wait_recv()
        cols = slice(j * piece, (j + 1) * piece)

        @pl.loop(0, positions // tile)
        def _(i):
            here = pl.ds(pl.multiple_of(i * tile, tile), tile)
            value = total[j, here, :] + product(here, j, (3, 7)) + ebias_ref[:, cols]
            out_ref[here, cols] = (
                0.5 * value * (1.0 + lax.erf(value * (1.0 / math.sqrt(2.0))))
            ).astype(jnp.bfloat16)

    for j in range(pieces):
        own_copy(j).wait()
        core_copy(0, j).wait_recv()
        core_copy(1, j).wait_recv()
    first(0)
    first(1)
    x_arrived(3)
    far_arrived(0)
    first(2)
    first(3)
    for j in range(pieces):
        second(j)
    far_arrived(1)
    third(0)
    far_arrived(2)
    third(1)
    far_arrived(3)
    third(2)
    third(3)

    @pl.loop(0, heads)
    def _(h):
        key_copy(h).wait_send()
        value_copy(h).wait_send()
        halo_copy(h).wait_send()

    for j in range(pieces):
        y_copy(j).wait_send()
        x_copy(j).wait_send()
        far_copy(j).wait_send()
        for b in range(4):
            core_copy(b, j).wait_send()


def on_device_kernel(
    planes,
    inputs,
    query_proj,
    key_proj,
    value_proj,
    depth_weight,
    depth_bias,
    norm_gain,
    norm_bias,
    expand_weight,
    expand_bias,
):
    _, rows, width, chans = inputs.shape
    positions, heads = rows * width, chans // HEAD_DIM
    depth, units = expand_weight.shape
    pieces = 4
    piece = units // pieces
    margin = KERNEL // 2

    def flat(array):
        return array.reshape(positions, chans)

    def wide(array, lead=1):
        return array.astype(jnp.float32).reshape(lead, -1)

    vmem, anywhere = pl.BlockSpec(memory_space=pltpu.VMEM), pl.BlockSpec(memory_space=pl.ANY)
    dma = pltpu.SemaphoreType.DMA
    residual, hidden = pl.pallas_call(
        functools.partial(whole_block, heads=heads, rows=rows, width=width, planes=planes),
        out_shape=(
            jax.ShapeDtypeStruct((positions, chans), jnp.bfloat16),
            jax.ShapeDtypeStruct((positions, units), jnp.bfloat16),
        ),
        in_specs=[vmem] * 8 + [anywhere, vmem],
        out_specs=(vmem, vmem),
        scratch_shapes=[
            pltpu.VMEM((heads, positions, HEAD_DIM), jnp.bfloat16),
            pltpu.VMEM((heads, positions, HEAD_DIM), jnp.bfloat16),
            pltpu.VMEM((heads, margin * width, HEAD_DIM), jnp.bfloat16),
            pltpu.VMEM(((rows + 2 * margin) * width, HEAD_DIM), jnp.float32),
            pltpu.VMEM((4, KERNEL, width + 16, HEAD_DIM), jnp.float32),
            pltpu.VMEM((positions, planes * chans), jnp.bfloat16),
            pltpu.VMEM((8, pieces, depth, piece), jnp.bfloat16),
            pltpu.VMEM((pieces, positions, piece), jnp.float32),
            dma((2 * heads,)), dma((2 * heads,)),
            dma((heads,)), dma((heads,)),
            dma(((planes - 1) * heads,)), dma(((planes - 1) * heads,)),
            dma((pieces,)),
            dma((pieces,)), dma((pieces,)),
            dma((pieces,)), dma((pieces,)),
            dma((pieces,)), dma((pieces,)),
            dma((4 * pieces,)), dma((4 * pieces,)),
        ],
        compiler_params=pltpu.CompilerParams(
            collective_id=0, has_side_effects=True, vmem_limit_bytes=VMEM_BYTES
        ),
    )(
        flat(inputs), flat(query_proj), flat(key_proj), flat(value_proj),
        wide(depth_weight, KERNEL * KERNEL), wide(depth_bias), wide(norm_gain), wide(norm_bias),
        expand_weight, wide(expand_bias),
    )
    return (residual.reshape(inputs.shape), hidden.reshape(1, rows, width, units))


def solution(mesh):
    body = on_device
    if mesh.shape["seq"] == 2 and mesh.shape["row"] == 4:
        body = functools.partial(on_device_kernel, mesh.shape["col"])
    return jax.shard_map(
        body,
        mesh=mesh,
        in_specs=(
            P("row", "seq", None, "col"),
            P("row", "seq", None, "col"),
            P("row", "seq", None, "col"),
            P("row", "seq", None, "col"),
            P(None, None, "col"),
            P("col"),
            P(),
            P(),
            P(("seq", "row"), "col"),
            P("col"),
        ),
        out_specs=(P("row", "seq", None, "col"), P("row", "seq", None, "col")),
        check_vma=False,
    )
```

```python
import functools
import math

import jax
import jax.numpy as jnp
from jax import lax
from jax.experimental import pallas as pl
from jax.experimental.pallas import tpu as pltpu
from jax.sharding import PartitionSpec as P

HEAD_DIM = 128
KERNEL = 7
VMEM_BYTES = 62 * 1024 * 1024


def padded_2(array, sides, width):
    for axis, dim in sides:
        peers, length = (lax.axis_size(axis), array.shape[dim])
        up = [(i, (i + 1) % peers) for i in range(peers - 1)]
        down = [(j, i) for i, j in up]
        last = lax.slice_in_dim(array, length - width, length, axis=dim)
        leading = lax.slice_in_dim(array, 0, width, axis=dim)
        before = lax.ppermute(last, axis, up)
        after = lax.ppermute(leading, axis, down)
        array = jnp.concatenate([before, array, after], axis=dim)
    return array


def on_device(
    inputs,
    query_proj,
    key_proj,
    value_proj,
    depth_weight,
    depth_bias,
    norm_gain,
    norm_bias,
    expand_weight,
    expand_bias,
):
    samples, rows_here, col_count, channels = inputs.shape
    heads_here = channels // HEAD_DIM
    positions = rows_here * col_count
    score_scale = 1.0 / math.sqrt(HEAD_DIM)
    queries = query_proj.reshape(samples, positions, heads_here, HEAD_DIM)
    start_max = jnp.full((samples, heads_here, positions), -1e30, jnp.float32)
    keys_in = lax.all_gather(key_proj, "seq", axis=1, tiled=True)
    values_in = lax.all_gather(value_proj, "seq", axis=1, tiled=True)
    count = keys_in.shape[1] * keys_in.shape[2]
    keys_in = keys_in.reshape(samples, count, heads_here, HEAD_DIM)
    values_in = values_in.reshape(samples, count, heads_here, HEAD_DIM)
    scores = (
        jnp.einsum("bqhd,bkhd->bhqk", queries, keys_in, preferred_element_type=jnp.float32)
        * score_scale
    )
    new_max = jnp.maximum(start_max, jnp.max(scores, axis=-1))
    weights = jnp.exp(scores - new_max[..., None])
    new_total = jnp.sum(weights, axis=-1)
    update = jnp.einsum(
        "bhqk,bkhd->bhqd",
        weights.astype(jnp.bfloat16),
        values_in,
        preferred_element_type=jnp.float32,
    )
    attended = update / new_total[..., None]
    attended = jnp.transpose(attended, (0, 2, 1, 3)).reshape(
        samples, rows_here, col_count, channels
    )
    residual_out = (inputs.astype(jnp.float32) + attended).astype(jnp.bfloat16)
    margin = KERNEL // 2
    padded = padded_2(residual_out, (("seq", 1),), margin)
    padded = jnp.pad(padded, ((0, 0), (0, 0), (margin, margin), (0, 0))).astype(jnp.float32)
    kernel_taps = depth_weight.astype(jnp.float32)
    convolved = jnp.zeros((samples, rows_here, col_count, channels), jnp.float32)
    for row_tap in range(KERNEL):
        for col_tap in range(KERNEL):
            convolved = (
                convolved
                + padded[:, row_tap : row_tap + rows_here, col_tap : col_tap + col_count, :]
                * kernel_taps[row_tap, col_tap]
            )
    convolved = (convolved + depth_bias.astype(jnp.float32)).astype(jnp.bfloat16)
    flat_rows = convolved.reshape(samples * positions, channels)
    gathered = lax.all_gather(flat_rows, "col", axis=1, tiled=True)
    widened = gathered.astype(jnp.float32)
    center = jnp.mean(widened, axis=1, keepdims=True)
    spread = jnp.mean((widened - center) * (widened - center), axis=1, keepdims=True)
    normed = (
        (widened - center) * lax.rsqrt(spread + 1e-06) * norm_gain.astype(jnp.float32)
        + norm_bias.astype(jnp.float32)
    ).astype(jnp.bfloat16)
    project = jnp.dot(
        normed,
        lax.all_gather(expand_weight, ("seq", "row"), axis=0, tiled=True),
        preferred_element_type=jnp.float32,
    )
    hidden = jax.nn.gelu(project + expand_bias.astype(jnp.float32), approximate=False).astype(
        jnp.bfloat16
    )
    return (residual_out, hidden.reshape(samples, rows_here, col_count, expand_weight.shape[1]))


def whole_block(
    x_ref, q_ref, k_ref, v_ref, taps_ref, vectors_ref, w_ref,
    res_ref, out_ref,
    k_in, v_in, halo, rows_f32, shifted, taps, acts, weights, total,
    kv_send, kv_recv, halo_send, halo_recv, z_send, z_recv, own_sem,
    y_send, y_recv, x_send, x_recv, far_send, far_recv, core_send, core_recv,
    *, heads, rows, width, planes,
):
    seq, row, col = (lax.axis_index(a) for a in ("seq", "row", "col"))
    positions = rows * width
    margin = KERNEL // 2
    strip = margin * width
    chans = heads * HEAD_DIM
    depth = w_ref.shape[0]
    pieces, piece = total.shape[0], total.shape[2]
    by_y, ahead, lag = pieces * 3 // 4, 3, 2
    to_x = {"seq": 1 - seq}
    to_y = {"row": lax.rem(row + 2, 4)}
    to_core = {"row": row + 1 - 2 * lax.rem(row, 2)}
    z_peers = [{"col": lax.rem(col + i, planes)} for i in range(1, planes)]

    def remote(src, dst, send, recv, where):
        return pltpu.make_async_remote_copy(
            src_ref=src, dst_ref=dst, send_sem=send, recv_sem=recv,
            device_id=where, device_id_type=pl.DeviceIdType.MESH,
        )

    def lanes(h):
        return pl.ds(pl.multiple_of(h * HEAD_DIM, HEAD_DIM), HEAD_DIM)

    def key_copy(h):
        return remote(k_ref.at[:, lanes(h)], k_in.at[h], kv_send.at[h], kv_recv.at[h], to_x)

    def value_copy(h):
        return remote(
            v_ref.at[:, lanes(h)], v_in.at[h], kv_send.at[heads + h], kv_recv.at[heads + h], to_x
        )

    def halo_copy(h):
        start = pl.multiple_of((1 - seq) * (positions - strip), width)
        return remote(
            res_ref.at[pl.ds(start, strip), lanes(h)], halo.at[h],
            halo_send.at[h], halo_recv.at[h], to_x,
        )

    def act_lanes(h, plane):
        return pl.ds(pl.multiple_of(plane * chans + h * HEAD_DIM, HEAD_DIM), HEAD_DIM)

    def act_copy(h, i):
        part = acts.at[:, act_lanes(h, col)]
        return remote(
            part, part, z_send.at[i * heads + h], z_recv.at[i * heads + h], z_peers[i]
        )

    def act_arrival(h, i):
        plane = lax.rem(col + planes - i - 1, planes)
        part = acts.at[:, act_lanes(h, plane)]
        return remote(
            part, part, z_send.at[i * heads + h], z_recv.at[i * heads + h], z_peers[i]
        )

    def own_piece(j):
        return w_ref.at[:, pl.ds(j * piece, piece)]

    def own_copy(j):
        return pltpu.make_async_copy(own_piece(j), weights.at[0, j], own_sem.at[j])

    def y_copy(j):
        return remote(own_piece(j), weights.at[1, j], y_send.at[j], y_recv.at[j], to_y)

    def x_copy(j):
        return remote(own_piece(j), weights.at[2, j], x_send.at[j], x_recv.at[j], to_x)

    def far_copy(j):
        if j < by_y:
            return remote(
                weights.at[2, j], weights.at[3, j], far_send.at[j], far_recv.at[j], to_y
            )
        return remote(weights.at[1, j], weights.at[3, j], far_send.at[j], far_recv.at[j], to_x)

    def core_copy(b, j):
        src = own_piece(j) if b == 0 else weights.at[b, j]
        at = b * pieces + j
        return remote(src, weights.at[4 + b, j], core_send.at[at], core_recv.at[at], to_core)

    barrier = pltpu.get_barrier_semaphore()
    peers = [to_x, to_y, to_core] + z_peers
    for peer in peers:
        pl.semaphore_signal(
            barrier, inc=1, device_id=peer, device_id_type=pl.DeviceIdType.MESH
        )
    pl.semaphore_wait(barrier, len(peers))

    for h in range(min(ahead, heads)):
        key_copy(h).start()
        value_copy(h).start()
    for j in range(pieces):
        y_copy(j).start()
    for j in range(pieces):
        own_copy(j).start()
        core_copy(0, j).start()

    scale = 1.0 / math.sqrt(HEAD_DIM)
    half = positions // 2
    shifted[...] = jnp.zeros_like(shifted)
    taps[...] = taps_ref[...].astype(jnp.float32)

    channels = acts.shape[1]
    gain_at, nbias_at = chans, chans + channels
    ebias_at = nbias_at + channels

    def vector(start, size):
        return vectors_ref[:, pl.ds(start, size)]

    def attend(h):
        keys, values = k_ref[:, lanes(h)], v_ref[:, lanes(h)]
        far_keys, far_values = k_in[h], v_in[h]
        over = (((1,), (1,)), ((), ()))

        @pl.loop(0, 2)
        def _(i):
            here = pl.ds(pl.multiple_of(i * half, half), half)
            queries = q_ref[here, lanes(h)]
            near = lax.dot_general(queries, keys, over, preferred_element_type=jnp.float32) * scale
            far = lax.dot_general(queries, far_keys, over, preferred_element_type=jnp.float32) * scale
            peak = jnp.maximum(
                jnp.max(near, axis=1, keepdims=True), jnp.max(far, axis=1, keepdims=True)
            )
            near, far = jnp.exp(near - peak), jnp.exp(far - peak)
            count = jnp.sum(near, axis=1, keepdims=True) + jnp.sum(far, axis=1, keepdims=True)
            mixed = jnp.dot(
                near.astype(jnp.bfloat16), values, preferred_element_type=jnp.float32
            ) + jnp.dot(far.astype(jnp.bfloat16), far_values, preferred_element_type=jnp.float32)
            res_ref[here, lanes(h)] = (
                x_ref[here, lanes(h)].astype(jnp.float32) + mixed / count
            ).astype(jnp.bfloat16)

    def convolve(h):
        edge = halo[h].astype(jnp.float32)
        lead, trail = margin * width, (margin + rows) * width
        rows_f32[0:lead, :] = jnp.where(seq == 1, edge, 0.0)
        rows_f32[lead:trail, :] = res_ref[:, lanes(h)].astype(jnp.float32)
        rows_f32[trail:, :] = jnp.where(seq == 0, edge, 0.0)
        group = 4

        @pl.loop(0, rows // group)
        def _(g):
            base = g * (group * width)
            for q in range(KERNEL):
                sums = [None] * group
                for r in range(group + KERNEL - 1):
                    start = pl.multiple_of(base + r * width, width)
                    line = rows_f32[pl.ds(start, width), :]
                    for o in range(group):
                        p = r - o
                        if 0 <= p < KERNEL:
                            term = line * taps[p, q : q + 1, lanes(h)]
                            sums[o] = term if sums[o] is None else sums[o] + term
                for o in range(group):
                    shifted[o, q, 8 : 8 + width, :] = sums[o]
            for o in range(group):
                value = shifted[o, margin, 8 : 8 + width, :] + vectors_ref[:, lanes(h)]
                for q in range(KERNEL):
                    if q != margin:
                        begin = 8 + q - margin
                        value = value + shifted[o, q, begin : begin + width, :]
                start = pl.multiple_of(base + o * width, width)
                acts[pl.ds(start, width), act_lanes(h, col)] = value.astype(jnp.bfloat16)

    def y_arrived(j):
        y_copy(j).wait_recv()
        core_copy(1, j).start()
        if j >= by_y:
            far_copy(j).start()

    def x_arrived(j):
        x_copy(j).wait_recv()
        if j < by_y:
            far_copy(j).start()
        core_copy(2, j).start()

    def far_arrived(j):
        far_copy(j).wait_recv()
        core_copy(3, j).start()

    @pl.loop(0, heads + lag)
    def _(h):
        @pl.when(h + ahead < heads)
        def _():
            key_copy(h + ahead).start()
            value_copy(h + ahead).start()

        for j, when in enumerate((2, 4, 6)):
            @pl.when(h == when)
            def _():
                x_copy(j).start()

        @pl.when(h < heads)
        def _():
            key_copy(h).wait_recv()
            value_copy(h).wait_recv()
            attend(h)
            halo_copy(h).start()

        @pl.when(h == heads)
        def _():
            for j in range(3, pieces):
                x_copy(j).start()
            for j in range(pieces):
                y_arrived(j)
            x_arrived(0)

        @pl.when(h == heads + 1)
        def _():
            x_arrived(1)

        @pl.when(h >= lag)
        def _():
            halo_copy(h - lag).wait_recv()
            convolve(h - lag)
            for i in range(planes - 1):
                act_copy(h - lag, i).start()

    x_arrived(2)

    @pl.loop(0, heads)
    def _(h):
        for i in range(planes - 1):
            act_arrival(h, i).wait_recv()
            act_copy(h, i).wait_send()

    x_arrived(3)
    block = 16
    inverse = 1.0 / acts.shape[1]

    @pl.loop(0, positions // block)
    def _(i):
        here = pl.ds(pl.multiple_of(i * block, block), block)
        wide = acts[here, :].astype(jnp.float32)
        center = jnp.sum(wide, axis=1, keepdims=True) * inverse
        wide = wide - center
        spread = jnp.sum(wide * wide, axis=1, keepdims=True) * inverse
        acts[here, :] = (
            wide * lax.rsqrt(spread + 1e-06) * vector(gain_at, channels) + vector(nbias_at, channels)
        ).astype(jnp.bfloat16)

    other = row + 1 - 2 * lax.rem(row, 2)
    places = []
    for r in (row, other):
        y = lax.rem(r + 2, 4)
        places.append([seq * 4 + r, seq * 4 + y, (1 - seq) * 4 + r, (1 - seq) * 4 + y])
    places = places[0] + places[1]

    def product(here, j, slots):
        result = None
        for slot in slots:
            cols = pl.ds(pl.multiple_of(places[slot] * depth, depth), depth)
            term = jnp.dot(
                acts[here, cols], weights[slot, j], preferred_element_type=jnp.float32
            )
            result = term if result is None else result + term
        return result

    tile = 256

    def first(j):
        @pl.loop(0, positions // tile)
        def _(i):
            here = pl.ds(pl.multiple_of(i * tile, tile), tile)
            total[j, here, :] = product(here, j, (0, 4, 1, 5))

    def second(j):
        core_copy(2, j).wait_recv()

        @pl.loop(0, positions // tile)
        def _(i):
            here = pl.ds(pl.multiple_of(i * tile, tile), tile)
            total[j, here, :] += product(here, j, (2, 6))

    def third(j):
        core_copy(3, j).wait_recv()
        cols = slice(j * piece, (j + 1) * piece)

        @pl.loop(0, positions // tile)
        def _(i):
            here = pl.ds(pl.multiple_of(i * tile, tile), tile)
            value = total[j, here, :] + product(here, j, (3, 7)) + vector(ebias_at + j * piece, piece)
            out_ref[here, cols] = (
                0.5 * value * (1.0 + lax.erf(value * (1.0 / math.sqrt(2.0))))
            ).astype(jnp.bfloat16)

    for j in range(pieces):
        own_copy(j).wait()
        core_copy(0, j).wait_recv()
        core_copy(1, j).wait_recv()
    for j in range(4):
        first(j)
    x_arrived(4)
    x_arrived(5)
    far_arrived(0)
    for j in range(4, pieces):
        first(j)
    x_arrived(6)
    far_arrived(1)
    for j in range(4):
        second(j)
    far_arrived(2)
    x_arrived(7)
    for j in range(4, pieces):
        second(j)
    for j in range(3, pieces):
        far_arrived(j)
        third(j - 3)
    for j in range(pieces - 3, pieces):
        third(j)

    @pl.loop(0, heads)
    def _(h):
        key_copy(h).wait_send()
        value_copy(h).wait_send()
        halo_copy(h).wait_send()

    for j in range(pieces):
        y_copy(j).wait_send()
        x_copy(j).wait_send()
        far_copy(j).wait_send()
        for b in range(4):
            core_copy(b, j).wait_send()


def on_device_kernel(
    planes,
    inputs,
    query_proj,
    key_proj,
    value_proj,
    depth_weight,
    depth_bias,
    norm_gain,
    norm_bias,
    expand_weight,
    expand_bias,
):
    _, rows, width, chans = inputs.shape
    positions, heads = rows * width, chans // HEAD_DIM
    depth, units = expand_weight.shape
    pieces = 8
    piece = units // pieces
    margin = KERNEL // 2

    def flat(array):
        return array.reshape(positions, chans)

    vectors = jnp.concatenate([depth_bias, norm_gain, norm_bias, expand_bias])
    vectors = lax.optimization_barrier(vectors.astype(jnp.float32)).reshape(1, -1)
    vmem, anywhere = pl.BlockSpec(memory_space=pltpu.VMEM), pl.BlockSpec(memory_space=pl.ANY)
    dma = pltpu.SemaphoreType.DMA
    residual, hidden = pl.pallas_call(
        functools.partial(whole_block, heads=heads, rows=rows, width=width, planes=planes),
        out_shape=(
            jax.ShapeDtypeStruct((positions, chans), jnp.bfloat16),
            jax.ShapeDtypeStruct((positions, units), jnp.bfloat16),
        ),
        in_specs=[vmem] * 6 + [anywhere],
        out_specs=(vmem, vmem),
        scratch_shapes=[
            pltpu.VMEM((heads, positions, HEAD_DIM), jnp.bfloat16),
            pltpu.VMEM((heads, positions, HEAD_DIM), jnp.bfloat16),
            pltpu.VMEM((heads, margin * width, HEAD_DIM), jnp.bfloat16),
            pltpu.VMEM(((rows + 2 * margin) * width, HEAD_DIM), jnp.float32),
            pltpu.VMEM((4, KERNEL, width + 16, HEAD_DIM), jnp.float32),
            pltpu.VMEM((KERNEL, KERNEL, chans), jnp.float32),
            pltpu.VMEM((positions, planes * chans), jnp.bfloat16),
            pltpu.VMEM((8, pieces, depth, piece), jnp.bfloat16),
            pltpu.VMEM((pieces, positions, piece), jnp.float32),
            dma((2 * heads,)), dma((2 * heads,)),
            dma((heads,)), dma((heads,)),
            dma(((planes - 1) * heads,)), dma(((planes - 1) * heads,)),
            dma((pieces,)),
            dma((pieces,)), dma((pieces,)),
            dma((pieces,)), dma((pieces,)),
            dma((pieces,)), dma((pieces,)),
            dma((4 * pieces,)), dma((4 * pieces,)),
        ],
        compiler_params=pltpu.CompilerParams(
            collective_id=0, has_side_effects=True, vmem_limit_bytes=VMEM_BYTES
        ),
    )(
        flat(inputs), flat(query_proj), flat(key_proj), flat(value_proj),
        depth_weight, vectors, expand_weight,
    )
    return (residual.reshape(inputs.shape), hidden.reshape(1, rows, width, units))


def solution(mesh):
    body = on_device
    if mesh.shape["seq"] == 2 and mesh.shape["row"] == 4:
        body = functools.partial(on_device_kernel, mesh.shape["col"])
    return jax.shard_map(
        body,
        mesh=mesh,
        in_specs=(
            P("row", "seq", None, "col"),
            P("row", "seq", None, "col"),
            P("row", "seq", None, "col"),
            P("row", "seq", None, "col"),
            P(None, None, "col"),
            P("col"),
            P(),
            P(),
            P(("seq", "row"), "col"),
            P("col"),
        ),
        out_specs=(P("row", "seq", None, "col"), P("row", "seq", None, "col")),
        check_vma=False,
    )
```

```python
import functools
import math

import jax
import jax.numpy as jnp
from jax import lax
from jax.experimental import pallas as pl
from jax.experimental.pallas import tpu as pltpu
from jax.sharding import PartitionSpec as P

HEAD_DIM = 128
KERNEL = 7
COPY_PARTS = 8
VMEM_BYTES = 62 * 1024 * 1024


def padded_2(array, sides, width):
    for axis, dim in sides:
        peers, length = (lax.axis_size(axis), array.shape[dim])
        up = [(i, (i + 1) % peers) for i in range(peers - 1)]
        down = [(j, i) for i, j in up]
        last = lax.slice_in_dim(array, length - width, length, axis=dim)
        leading = lax.slice_in_dim(array, 0, width, axis=dim)
        before = lax.ppermute(last, axis, up)
        after = lax.ppermute(leading, axis, down)
        array = jnp.concatenate([before, array, after], axis=dim)
    return array


def on_device(
    inputs,
    query_proj,
    key_proj,
    value_proj,
    depth_weight,
    depth_bias,
    norm_gain,
    norm_bias,
    expand_weight,
    expand_bias,
):
    samples, rows_here, col_count, channels = inputs.shape
    heads_here = channels // HEAD_DIM
    positions = rows_here * col_count
    score_scale = 1.0 / math.sqrt(HEAD_DIM)
    queries = query_proj.reshape(samples, positions, heads_here, HEAD_DIM)
    start_max = jnp.full((samples, heads_here, positions), -1e30, jnp.float32)
    keys_in = lax.all_gather(key_proj, "seq", axis=1, tiled=True)
    values_in = lax.all_gather(value_proj, "seq", axis=1, tiled=True)
    count = keys_in.shape[1] * keys_in.shape[2]
    keys_in = keys_in.reshape(samples, count, heads_here, HEAD_DIM)
    values_in = values_in.reshape(samples, count, heads_here, HEAD_DIM)
    scores = (
        jnp.einsum("bqhd,bkhd->bhqk", queries, keys_in, preferred_element_type=jnp.float32)
        * score_scale
    )
    new_max = jnp.maximum(start_max, jnp.max(scores, axis=-1))
    weights = jnp.exp(scores - new_max[..., None])
    new_total = jnp.sum(weights, axis=-1)
    update = jnp.einsum(
        "bhqk,bkhd->bhqd",
        weights.astype(jnp.bfloat16),
        values_in,
        preferred_element_type=jnp.float32,
    )
    attended = update / new_total[..., None]
    attended = jnp.transpose(attended, (0, 2, 1, 3)).reshape(
        samples, rows_here, col_count, channels
    )
    residual_out = (inputs.astype(jnp.float32) + attended).astype(jnp.bfloat16)
    margin = KERNEL // 2
    padded = padded_2(residual_out, (("seq", 1),), margin)
    padded = jnp.pad(padded, ((0, 0), (0, 0), (margin, margin), (0, 0))).astype(jnp.float32)
    kernel_taps = depth_weight.astype(jnp.float32)
    convolved = jnp.zeros((samples, rows_here, col_count, channels), jnp.float32)
    for row_tap in range(KERNEL):
        for col_tap in range(KERNEL):
            convolved = (
                convolved
                + padded[:, row_tap : row_tap + rows_here, col_tap : col_tap + col_count, :]
                * kernel_taps[row_tap, col_tap]
            )
    convolved = (convolved + depth_bias.astype(jnp.float32)).astype(jnp.bfloat16)
    flat_rows = convolved.reshape(samples * positions, channels)
    gathered = lax.all_gather(flat_rows, "col", axis=1, tiled=True)
    widened = gathered.astype(jnp.float32)
    center = jnp.mean(widened, axis=1, keepdims=True)
    spread = jnp.mean((widened - center) * (widened - center), axis=1, keepdims=True)
    normed = (
        (widened - center) * lax.rsqrt(spread + 1e-06) * norm_gain.astype(jnp.float32)
        + norm_bias.astype(jnp.float32)
    ).astype(jnp.bfloat16)
    project = jnp.dot(
        normed,
        lax.all_gather(expand_weight, ("seq", "row"), axis=0, tiled=True),
        preferred_element_type=jnp.float32,
    )
    hidden = jax.nn.gelu(project + expand_bias.astype(jnp.float32), approximate=False).astype(
        jnp.bfloat16
    )
    return (residual_out, hidden.reshape(samples, rows_here, col_count, expand_weight.shape[1]))


def whole_block(
    x_hbm, q_hbm, k_hbm, v_hbm, taps_ref, vectors_ref, w_ref,
    res_hbm, out_hbm,
    x_ref, q_ref, k_ref, v_ref, res_ref, out_ref,
    k_in, v_in, halo, rows_f32, shifted, taps, acts, weights, total,
    in_sem, res_sem, out_sem, kv_send, kv_recv, halo_send, halo_recv, z_send, z_recv, own_sem,
    y_send, y_recv, x_send, x_recv, far_send, far_recv, core_send, core_recv,
    *, heads, rows, width, planes,
):
    seq, row, col = (lax.axis_index(a) for a in ("seq", "row", "col"))
    positions = rows * width
    margin = KERNEL // 2
    strip = margin * width
    chans = heads * HEAD_DIM
    depth = w_ref.shape[0]
    pieces, piece = total.shape[0], total.shape[2]
    by_y, ahead, lag = pieces * 3 // 4, 3, 2
    to_x = {"seq": 1 - seq}
    to_y = {"row": lax.rem(row + 2, 4)}
    to_core = {"row": row + 1 - 2 * lax.rem(row, 2)}
    z_peers = [{"col": lax.rem(col + i, planes)} for i in range(1, planes)]

    def remote(src, dst, send, recv, where):
        return pltpu.make_async_remote_copy(
            src_ref=src, dst_ref=dst, send_sem=send, recv_sem=recv,
            device_id=where, device_id_type=pl.DeviceIdType.MESH,
        )

    def lanes(h):
        return pl.ds(pl.multiple_of(h * HEAD_DIM, HEAD_DIM), HEAD_DIM)

    def key_copy(h):
        return remote(k_hbm.at[:, lanes(h)], k_in.at[h], kv_send.at[h], kv_recv.at[h], to_x)

    def value_copy(h):
        return remote(
            v_hbm.at[:, lanes(h)], v_in.at[h], kv_send.at[heads + h], kv_recv.at[heads + h], to_x
        )

    def halo_copy(h):
        start = pl.multiple_of((1 - seq) * (positions - strip), width)
        return remote(
            res_ref.at[pl.ds(start, strip), lanes(h)], halo.at[h],
            halo_send.at[h], halo_recv.at[h], to_x,
        )

    def act_lanes(h, plane):
        return pl.ds(pl.multiple_of(plane * chans + h * HEAD_DIM, HEAD_DIM), HEAD_DIM)

    def act_copy(h, i):
        part = acts.at[:, act_lanes(h, col)]
        return remote(
            part, part, z_send.at[i * heads + h], z_recv.at[i * heads + h], z_peers[i]
        )

    def act_arrival(h, i):
        plane = lax.rem(col + planes - i - 1, planes)
        part = acts.at[:, act_lanes(h, plane)]
        return remote(
            part, part, z_send.at[i * heads + h], z_recv.at[i * heads + h], z_peers[i]
        )

    def own_piece(j):
        return w_ref.at[:, pl.ds(j * piece, piece)]

    def own_copy(j):
        return pltpu.make_async_copy(own_piece(j), weights.at[0, j], own_sem.at[j])

    def y_copy(j):
        return remote(own_piece(j), weights.at[1, j], y_send.at[j], y_recv.at[j], to_y)

    def x_copy(j):
        return remote(own_piece(j), weights.at[2, j], x_send.at[j], x_recv.at[j], to_x)

    def far_part(j, rows_here, at, over_y):
        src, where = (2, to_y) if over_y else (1, to_x)
        return remote(
            weights.at[src, j, rows_here], weights.at[3, j, rows_here],
            far_send.at[at], far_recv.at[at], where,
        )

    def far_y(j):
        if j == by_y:
            return [far_part(j, pl.ds(0, depth // 2), j, True)]
        return [far_part(j, pl.ds(0, depth), j, True)] if j < by_y else []

    def far_x(j):
        if j == by_y:
            return [far_part(j, pl.ds(depth // 2, depth // 2), pieces, False)]
        return [far_part(j, pl.ds(0, depth), j, False)] if j > by_y else []

    def core_copy(b, j):
        src = own_piece(j) if b == 0 else weights.at[b, j]
        at = b * pieces + j
        return remote(src, weights.at[4 + b, j], core_send.at[at], core_recv.at[at], to_core)

    locals_in = [
        pltpu.make_async_copy(src, dst, in_sem.at[i])
        for i, (src, dst) in enumerate(
            ((q_hbm, q_ref), (k_hbm, k_ref), (v_hbm, v_ref), (x_hbm, x_ref))
        )
    ]
    res_copy = pltpu.make_async_copy(res_ref, res_hbm, res_sem.at[0])

    def out_copy(j):
        part = (slice(None), pl.ds(j * piece, piece))
        return pltpu.make_async_copy(out_ref.at[part], out_hbm.at[part], out_sem.at[j])

    for copy in locals_in:
        copy.start()
    barrier = pltpu.get_barrier_semaphore()
    peers = [to_x, to_y, to_core] + z_peers
    for peer in peers:
        pl.semaphore_signal(
            barrier, inc=1, device_id=peer, device_id_type=pl.DeviceIdType.MESH
        )
    pl.semaphore_wait(barrier, len(peers))

    for h in range(min(ahead, heads)):
        key_copy(h).start()
        value_copy(h).start()
    for j in range(pieces):
        y_copy(j).start()
    for j in range(pieces):
        own_copy(j).start()
        core_copy(0, j).start()

    scale = 1.0 / math.sqrt(HEAD_DIM)
    half = positions // 2
    shifted[...] = jnp.zeros_like(shifted)
    taps[...] = taps_ref[...].astype(jnp.float32)

    for copy in locals_in:
        copy.wait()
    channels = acts.shape[1]
    gain_at, nbias_at = chans, chans + channels
    ebias_at = nbias_at + channels

    def vector(start, size):
        return vectors_ref[:, pl.ds(start, size)]

    def attend(h):
        keys, values = k_ref[:, lanes(h)], v_ref[:, lanes(h)]
        far_keys, far_values = k_in[h], v_in[h]
        over = (((1,), (1,)), ((), ()))

        @pl.loop(0, 2)
        def _(i):
            here = pl.ds(pl.multiple_of(i * half, half), half)
            queries = q_ref[here, lanes(h)]
            near = lax.dot_general(queries, keys, over, preferred_element_type=jnp.float32) * scale
            far = lax.dot_general(queries, far_keys, over, preferred_element_type=jnp.float32) * scale
            peak = jnp.maximum(
                jnp.max(near, axis=1, keepdims=True), jnp.max(far, axis=1, keepdims=True)
            )
            near, far = jnp.exp(near - peak), jnp.exp(far - peak)
            count = jnp.sum(near, axis=1, keepdims=True) + jnp.sum(far, axis=1, keepdims=True)
            mixed = jnp.dot(
                near.astype(jnp.bfloat16), values, preferred_element_type=jnp.float32
            ) + jnp.dot(far.astype(jnp.bfloat16), far_values, preferred_element_type=jnp.float32)
            res_ref[here, lanes(h)] = (
                x_ref[here, lanes(h)].astype(jnp.float32) + mixed / count
            ).astype(jnp.bfloat16)

    def convolve(h):
        edge = halo[h].astype(jnp.float32)
        lead, trail = margin * width, (margin + rows) * width
        rows_f32[0:lead, :] = jnp.where(seq == 1, edge, 0.0)
        rows_f32[lead:trail, :] = res_ref[:, lanes(h)].astype(jnp.float32)
        rows_f32[trail:, :] = jnp.where(seq == 0, edge, 0.0)
        group = 4

        @pl.loop(0, rows // group)
        def _(g):
            base = g * (group * width)
            for q in range(KERNEL):
                sums = [None] * group
                for r in range(group + KERNEL - 1):
                    start = pl.multiple_of(base + r * width, width)
                    line = rows_f32[pl.ds(start, width), :]
                    for o in range(group):
                        p = r - o
                        if 0 <= p < KERNEL:
                            term = line * taps[p, q : q + 1, lanes(h)]
                            sums[o] = term if sums[o] is None else sums[o] + term
                for o in range(group):
                    shifted[o, q, 8 : 8 + width, :] = sums[o]
            for o in range(group):
                value = shifted[o, margin, 8 : 8 + width, :] + vectors_ref[:, lanes(h)]
                for q in range(KERNEL):
                    if q != margin:
                        begin = 8 + q - margin
                        value = value + shifted[o, q, begin : begin + width, :]
                start = pl.multiple_of(base + o * width, width)
                acts[pl.ds(start, width), act_lanes(h, col)] = value.astype(jnp.bfloat16)

    def y_arrived(j):
        y_copy(j).wait_recv()
        core_copy(1, j).start()
        for part in far_x(j):
            part.start()

    def x_arrived(j):
        x_copy(j).wait_recv()
        for part in far_y(j):
            part.start()
        core_copy(2, j).start()

    def far_arrived(j):
        for part in far_y(j) + far_x(j):
            part.wait_recv()
        core_copy(3, j).start()

    @pl.loop(0, heads + lag)
    def _(h):
        @pl.when(h + ahead < heads)
        def _():
            key_copy(h + ahead).start()
            value_copy(h + ahead).start()

        for j, when in enumerate((2, 4, 6)):
            @pl.when(h == when)
            def _():
                x_copy(j).start()

        @pl.when(h < heads)
        def _():
            key_copy(h).wait_recv()
            value_copy(h).wait_recv()
            attend(h)
            halo_copy(h).start()

        @pl.when(h == heads)
        def _():
            for j in range(3, pieces):
                x_copy(j).start()

        @pl.when(h >= lag)
        def _():
            halo_copy(h - lag).wait_recv()
            convolve(h - lag)
            for i in range(planes - 1):
                act_copy(h - lag, i).start()

    res_copy.start()
    for j in range(5):
        y_arrived(j)
    x_arrived(0)
    y_arrived(5)
    x_arrived(1)
    y_arrived(6)
    x_arrived(2)
    y_arrived(7)

    @pl.loop(0, heads)
    def _(h):
        for i in range(planes - 1):
            act_arrival(h, i).wait_recv()
            act_copy(h, i).wait_send()

    x_arrived(3)
    block = 16
    inverse = 1.0 / acts.shape[1]

    @pl.loop(0, positions // block)
    def _(i):
        here = pl.ds(pl.multiple_of(i * block, block), block)
        wide = acts[here, :].astype(jnp.float32)
        center = jnp.sum(wide, axis=1, keepdims=True) * inverse
        wide = wide - center
        spread = jnp.sum(wide * wide, axis=1, keepdims=True) * inverse
        acts[here, :] = (
            wide * lax.rsqrt(spread + 1e-06) * vector(gain_at, channels) + vector(nbias_at, channels)
        ).astype(jnp.bfloat16)

    other = row + 1 - 2 * lax.rem(row, 2)
    places = []
    for r in (row, other):
        y = lax.rem(r + 2, 4)
        places.append([seq * 4 + r, seq * 4 + y, (1 - seq) * 4 + r, (1 - seq) * 4 + y])
    places = places[0] + places[1]

    def product(here, j, slots):
        result = None
        for slot in slots:
            cols = pl.ds(pl.multiple_of(places[slot] * depth, depth), depth)
            term = jnp.dot(
                acts[here, cols], weights[slot, j], preferred_element_type=jnp.float32
            )
            result = term if result is None else result + term
        return result

    tile = 256

    def first(j):
        @pl.loop(0, positions // tile)
        def _(i):
            here = pl.ds(pl.multiple_of(i * tile, tile), tile)
            total[j, here, :] = product(here, j, (0, 4, 1, 5))

    def second(j):
        core_copy(2, j).wait_recv()

        @pl.loop(0, positions // tile)
        def _(i):
            here = pl.ds(pl.multiple_of(i * tile, tile), tile)
            total[j, here, :] += product(here, j, (2, 6))

    def third(j):
        core_copy(3, j).wait_recv()
        cols = slice(j * piece, (j + 1) * piece)

        @pl.loop(0, positions // tile)
        def _(i):
            here = pl.ds(pl.multiple_of(i * tile, tile), tile)
            value = total[j, here, :] + product(here, j, (3, 7)) + vector(ebias_at + j * piece, piece)
            out_ref[here, cols] = (
                0.5 * value * (1.0 + lax.erf(value * (1.0 / math.sqrt(2.0))))
            ).astype(jnp.bfloat16)

        out_copy(j).start()

    for j in range(pieces):
        own_copy(j).wait()
        core_copy(0, j).wait_recv()
        core_copy(1, j).wait_recv()
    for j in range(4):
        first(j)
    x_arrived(4)
    x_arrived(5)
    far_arrived(0)
    for j in range(4, pieces):
        first(j)
    x_arrived(6)
    far_arrived(1)
    for j in range(4):
        second(j)
    far_arrived(2)
    x_arrived(7)
    for j in range(4, pieces):
        second(j)
    third(0)
    third(1)
    for j in range(3, pieces):
        far_arrived(j)
        third(j - 1)
    third(pieces - 1)
    res_copy.wait()

    @pl.loop(0, heads)
    def _(h):
        key_copy(h).wait_send()
        value_copy(h).wait_send()
        halo_copy(h).wait_send()

    for j in range(pieces):
        y_copy(j).wait_send()
        x_copy(j).wait_send()
        for part in far_y(j) + far_x(j):
            part.wait_send()
        out_copy(j).wait()
        for b in range(4):
            core_copy(b, j).wait_send()


def copy_out(res_in, out_in, res_ref, out_ref, sem):
    copies = []
    for i, (src, dst) in enumerate(((out_in, out_ref), (res_in, res_ref))):
        size = src.shape[0] // COPY_PARTS
        for n in range(COPY_PARTS):
            part = pl.ds(n * size, size)
            copies.append(
                pltpu.make_async_copy(src.at[part], dst.at[part], sem.at[i * COPY_PARTS + n])
            )
    for copy in copies:
        copy.start()
    for copy in copies:
        copy.wait()


def on_device_kernel(
    planes,
    inputs,
    query_proj,
    key_proj,
    value_proj,
    depth_weight,
    depth_bias,
    norm_gain,
    norm_bias,
    expand_weight,
    expand_bias,
):
    _, rows, width, chans = inputs.shape
    positions, heads = rows * width, chans // HEAD_DIM
    depth, units = expand_weight.shape
    pieces = 8
    piece = units // pieces
    margin = KERNEL // 2

    def flat(array):
        return array.reshape(positions, chans)

    vectors = jnp.concatenate([depth_bias, norm_gain, norm_bias, expand_bias])
    vectors = lax.optimization_barrier(vectors.astype(jnp.float32)).reshape(1, -1)
    vmem, anywhere = pl.BlockSpec(memory_space=pltpu.VMEM), pl.BlockSpec(memory_space=pl.ANY)
    dma = pltpu.SemaphoreType.DMA
    residual, hidden = pl.pallas_call(
        functools.partial(whole_block, heads=heads, rows=rows, width=width, planes=planes),
        out_shape=(
            jax.ShapeDtypeStruct((positions, chans), jnp.bfloat16),
            jax.ShapeDtypeStruct((positions, units), jnp.bfloat16),
        ),
        in_specs=[anywhere] * 4 + [vmem] * 2 + [anywhere],
        out_specs=(anywhere, anywhere),
        scratch_shapes=[
            *[pltpu.VMEM((positions, chans), jnp.bfloat16)] * 5,
            pltpu.VMEM((positions, units), jnp.bfloat16),
            pltpu.VMEM((heads, positions, HEAD_DIM), jnp.bfloat16),
            pltpu.VMEM((heads, positions, HEAD_DIM), jnp.bfloat16),
            pltpu.VMEM((heads, margin * width, HEAD_DIM), jnp.bfloat16),
            pltpu.VMEM(((rows + 2 * margin) * width, HEAD_DIM), jnp.float32),
            pltpu.VMEM((4, KERNEL, width + 16, HEAD_DIM), jnp.float32),
            pltpu.VMEM((KERNEL, KERNEL, chans), jnp.float32),
            pltpu.VMEM((positions, planes * chans), jnp.bfloat16),
            pltpu.VMEM((8, pieces, depth, piece), jnp.bfloat16),
            pltpu.VMEM((pieces, positions, piece), jnp.float32),
            dma((4,)), dma((1,)), dma((pieces,)),
            dma((2 * heads,)), dma((2 * heads,)),
            dma((heads,)), dma((heads,)),
            dma(((planes - 1) * heads,)), dma(((planes - 1) * heads,)),
            dma((pieces,)),
            dma((pieces,)), dma((pieces,)),
            dma((pieces,)), dma((pieces,)),
            dma((pieces + 1,)), dma((pieces + 1,)),
            dma((4 * pieces,)), dma((4 * pieces,)),
        ],
        compiler_params=pltpu.CompilerParams(
            collective_id=0, has_side_effects=True, vmem_limit_bytes=VMEM_BYTES
        ),
    )(
        flat(inputs), flat(query_proj), flat(key_proj), flat(value_proj),
        depth_weight, vectors, expand_weight,
    )
    residual, hidden = pl.pallas_call(
        copy_out,
        out_shape=(
            jax.ShapeDtypeStruct((positions, chans), jnp.bfloat16),
            jax.ShapeDtypeStruct((positions, units), jnp.bfloat16),
        ),
        in_specs=[anywhere] * 2,
        out_specs=(anywhere, anywhere),
        scratch_shapes=[dma((2 * COPY_PARTS,))],
        compiler_params=pltpu.CompilerParams(vmem_limit_bytes=VMEM_BYTES),
    )(residual, hidden)
    return (residual.reshape(inputs.shape), hidden.reshape(1, rows, width, units))


def solution(mesh):
    body = on_device
    if mesh.shape["seq"] == 2 and mesh.shape["row"] == 4:
        body = functools.partial(on_device_kernel, mesh.shape["col"])
    return jax.shard_map(
        body,
        mesh=mesh,
        in_specs=(
            P("row", "seq", None, "col"),
            P("row", "seq", None, "col"),
            P("row", "seq", None, "col"),
            P("row", "seq", None, "col"),
            P(None, None, "col"),
            P("col"),
            P(),
            P(),
            P(("seq", "row"), "col"),
            P("col"),
        ),
        out_specs=(P("row", "seq", None, "col"), P("row", "seq", None, "col")),
        check_vma=False,
    )
```

```python
import functools
import math

import jax
import jax.numpy as jnp
from jax import lax
from jax.experimental import pallas as pl
from jax.experimental.pallas import tpu as pltpu
from jax.sharding import PartitionSpec as P

HEAD_DIM = 128
KERNEL = 7
COPY_PARTS = 8
VMEM_BYTES = 62 * 1024 * 1024


def padded_2(array, sides, width):
    for axis, dim in sides:
        peers, length = (lax.axis_size(axis), array.shape[dim])
        up = [(i, (i + 1) % peers) for i in range(peers - 1)]
        down = [(j, i) for i, j in up]
        last = lax.slice_in_dim(array, length - width, length, axis=dim)
        leading = lax.slice_in_dim(array, 0, width, axis=dim)
        before = lax.ppermute(last, axis, up)
        after = lax.ppermute(leading, axis, down)
        array = jnp.concatenate([before, array, after], axis=dim)
    return array


def on_device(
    inputs,
    query_proj,
    key_proj,
    value_proj,
    depth_weight,
    depth_bias,
    norm_gain,
    norm_bias,
    expand_weight,
    expand_bias,
):
    samples, rows_here, col_count, channels = inputs.shape
    heads_here = channels // HEAD_DIM
    positions = rows_here * col_count
    score_scale = 1.0 / math.sqrt(HEAD_DIM)
    queries = query_proj.reshape(samples, positions, heads_here, HEAD_DIM)
    start_max = jnp.full((samples, heads_here, positions), -1e30, jnp.float32)
    keys_in = lax.all_gather(key_proj, "seq", axis=1, tiled=True)
    values_in = lax.all_gather(value_proj, "seq", axis=1, tiled=True)
    count = keys_in.shape[1] * keys_in.shape[2]
    keys_in = keys_in.reshape(samples, count, heads_here, HEAD_DIM)
    values_in = values_in.reshape(samples, count, heads_here, HEAD_DIM)
    scores = (
        jnp.einsum("bqhd,bkhd->bhqk", queries, keys_in, preferred_element_type=jnp.float32)
        * score_scale
    )
    new_max = jnp.maximum(start_max, jnp.max(scores, axis=-1))
    weights = jnp.exp(scores - new_max[..., None])
    new_total = jnp.sum(weights, axis=-1)
    update = jnp.einsum(
        "bhqk,bkhd->bhqd",
        weights.astype(jnp.bfloat16),
        values_in,
        preferred_element_type=jnp.float32,
    )
    attended = update / new_total[..., None]
    attended = jnp.transpose(attended, (0, 2, 1, 3)).reshape(
        samples, rows_here, col_count, channels
    )
    residual_out = (inputs.astype(jnp.float32) + attended).astype(jnp.bfloat16)
    margin = KERNEL // 2
    padded = padded_2(residual_out, (("seq", 1),), margin)
    padded = jnp.pad(padded, ((0, 0), (0, 0), (margin, margin), (0, 0))).astype(jnp.float32)
    kernel_taps = depth_weight.astype(jnp.float32)
    convolved = jnp.zeros((samples, rows_here, col_count, channels), jnp.float32)
    for row_tap in range(KERNEL):
        for col_tap in range(KERNEL):
            convolved = (
                convolved
                + padded[:, row_tap : row_tap + rows_here, col_tap : col_tap + col_count, :]
                * kernel_taps[row_tap, col_tap]
            )
    convolved = (convolved + depth_bias.astype(jnp.float32)).astype(jnp.bfloat16)
    flat_rows = convolved.reshape(samples * positions, channels)
    gathered = lax.all_gather(flat_rows, "col", axis=1, tiled=True)
    widened = gathered.astype(jnp.float32)
    center = jnp.mean(widened, axis=1, keepdims=True)
    spread = jnp.mean((widened - center) * (widened - center), axis=1, keepdims=True)
    normed = (
        (widened - center) * lax.rsqrt(spread + 1e-06) * norm_gain.astype(jnp.float32)
        + norm_bias.astype(jnp.float32)
    ).astype(jnp.bfloat16)
    project = jnp.dot(
        normed,
        lax.all_gather(expand_weight, ("seq", "row"), axis=0, tiled=True),
        preferred_element_type=jnp.float32,
    )
    hidden = jax.nn.gelu(project + expand_bias.astype(jnp.float32), approximate=False).astype(
        jnp.bfloat16
    )
    return (residual_out, hidden.reshape(samples, rows_here, col_count, expand_weight.shape[1]))


def whole_block(
    x_hbm, q_hbm, k_hbm, v_hbm, taps_ref, vectors_ref, w_ref,
    res_hbm, out_hbm,
    x_ref, q_ref, k_ref, v_ref, res_ref, out_ref,
    k_in, v_in, halo, rows_f32, shifted, taps, acts, weights, total,
    in_sem, res_sem, out_sem, kv_send, kv_recv, halo_send, halo_recv, z_send, z_recv, own_sem,
    y_send, y_recv, x_send, x_recv, far_send, far_recv, core_send, core_recv,
    *, heads, rows, width, planes,
):
    seq, row, col = (lax.axis_index(a) for a in ("seq", "row", "col"))
    positions = rows * width
    margin = KERNEL // 2
    strip = margin * width
    chans = heads * HEAD_DIM
    depth = w_ref.shape[0]
    pieces, piece = total.shape[0], total.shape[2]
    by_y, ahead, lag = pieces * 3 // 4, 3, 2
    to_x = {"seq": 1 - seq}
    to_y = {"row": lax.rem(row + 2, 4)}
    to_core = {"row": row + 1 - 2 * lax.rem(row, 2)}
    z_peers = [{"col": lax.rem(col + i, planes)} for i in range(1, planes)]

    def remote(src, dst, send, recv, where):
        return pltpu.make_async_remote_copy(
            src_ref=src, dst_ref=dst, send_sem=send, recv_sem=recv,
            device_id=where, device_id_type=pl.DeviceIdType.MESH,
        )

    def lanes(h):
        return pl.ds(pl.multiple_of(h * HEAD_DIM, HEAD_DIM), HEAD_DIM)

    def key_copy(h):
        return remote(k_hbm.at[:, lanes(h)], k_in.at[h], kv_send.at[h], kv_recv.at[h], to_x)

    def value_copy(h):
        return remote(
            v_hbm.at[:, lanes(h)], v_in.at[h], kv_send.at[heads + h], kv_recv.at[heads + h], to_x
        )

    def halo_copy(h):
        start = pl.multiple_of((1 - seq) * (positions - strip), width)
        return remote(
            res_ref.at[pl.ds(start, strip), lanes(h)], halo.at[h],
            halo_send.at[h], halo_recv.at[h], to_x,
        )

    def act_lanes(h, plane):
        return pl.ds(pl.multiple_of(plane * chans + h * HEAD_DIM, HEAD_DIM), HEAD_DIM)

    def act_copy(h, i):
        part = acts.at[:, act_lanes(h, col)]
        return remote(
            part, part, z_send.at[i * heads + h], z_recv.at[i * heads + h], z_peers[i]
        )

    def act_arrival(h, i):
        plane = lax.rem(col + planes - i - 1, planes)
        part = acts.at[:, act_lanes(h, plane)]
        return remote(
            part, part, z_send.at[i * heads + h], z_recv.at[i * heads + h], z_peers[i]
        )

    def own_piece(j):
        return w_ref.at[:, pl.ds(j * piece, piece)]

    def own_copy(j):
        return pltpu.make_async_copy(own_piece(j), weights.at[0, j], own_sem.at[j])

    def y_copy(j):
        return remote(weights.at[0, j], weights.at[1, j], y_send.at[j], y_recv.at[j], to_y)

    def x_copy(j):
        return remote(weights.at[0, j], weights.at[2, j], x_send.at[j], x_recv.at[j], to_x)

    def far_part(j, rows_here, at, over_y):
        src, where = (2, to_y) if over_y else (1, to_x)
        return remote(
            weights.at[src, j, rows_here], weights.at[3, j, rows_here],
            far_send.at[at], far_recv.at[at], where,
        )

    def far_y(j):
        if j == by_y:
            return [far_part(j, pl.ds(0, depth // 2), j, True)]
        return [far_part(j, pl.ds(0, depth), j, True)] if j < by_y else []

    def far_x(j):
        if j == by_y:
            return [far_part(j, pl.ds(depth // 2, depth // 2), pieces, False)]
        return [far_part(j, pl.ds(0, depth), j, False)] if j > by_y else []

    def core_copy(b, j):
        at = b * pieces + j
        return remote(weights.at[b, j], weights.at[4 + b, j], core_send.at[at], core_recv.at[at], to_core)

    locals_in = [
        pltpu.make_async_copy(src, dst, in_sem.at[i])
        for i, (src, dst) in enumerate(
            ((q_hbm, q_ref), (k_hbm, k_ref), (v_hbm, v_ref), (x_hbm, x_ref))
        )
    ]
    res_copy = pltpu.make_async_copy(res_ref, res_hbm, res_sem.at[0])

    def out_copy(j):
        part = (slice(None), pl.ds(j * piece, piece))
        return pltpu.make_async_copy(out_ref.at[part], out_hbm.at[part], out_sem.at[j])

    for copy in locals_in:
        copy.start()
    for j in range(pieces):
        own_copy(j).start()
    barrier = pltpu.get_barrier_semaphore()
    peers = [to_x, to_y, to_core] + z_peers
    for peer in peers:
        pl.semaphore_signal(
            barrier, inc=1, device_id=peer, device_id_type=pl.DeviceIdType.MESH
        )
    pl.semaphore_wait(barrier, len(peers))

    for h in range(min(ahead, heads)):
        key_copy(h).start()
        value_copy(h).start()
    for j in range(pieces):
        own_copy(j).wait()
        y_copy(j).start()
        core_copy(0, j).start()

    scale = 1.0 / math.sqrt(HEAD_DIM)
    half = positions // 2
    shifted[...] = jnp.zeros_like(shifted)
    taps[...] = taps_ref[...].astype(jnp.float32)

    for copy in locals_in:
        copy.wait()
    channels = acts.shape[1]
    gain_at, nbias_at = chans, chans + channels
    ebias_at = nbias_at + channels

    def vector(start, size):
        return vectors_ref[:, pl.ds(start, size)]

    def attend(h):
        keys, values = k_ref[:, lanes(h)], v_ref[:, lanes(h)]
        far_keys, far_values = k_in[h], v_in[h]
        over = (((1,), (1,)), ((), ()))

        @pl.loop(0, 2)
        def _(i):
            here = pl.ds(pl.multiple_of(i * half, half), half)
            queries = q_ref[here, lanes(h)]
            near = lax.dot_general(queries, keys, over, preferred_element_type=jnp.float32) * scale
            far = lax.dot_general(queries, far_keys, over, preferred_element_type=jnp.float32) * scale
            peak = jnp.maximum(
                jnp.max(near, axis=1, keepdims=True), jnp.max(far, axis=1, keepdims=True)
            )
            near, far = jnp.exp(near - peak), jnp.exp(far - peak)
            count = jnp.sum(near, axis=1, keepdims=True) + jnp.sum(far, axis=1, keepdims=True)
            mixed = jnp.dot(
                near.astype(jnp.bfloat16), values, preferred_element_type=jnp.float32
            ) + jnp.dot(far.astype(jnp.bfloat16), far_values, preferred_element_type=jnp.float32)
            res_ref[here, lanes(h)] = (
                x_ref[here, lanes(h)].astype(jnp.float32) + mixed / count
            ).astype(jnp.bfloat16)

    def convolve(h):
        edge = halo[h].astype(jnp.float32)
        lead, trail = margin * width, (margin + rows) * width
        rows_f32[0:lead, :] = jnp.where(seq == 1, edge, 0.0)
        rows_f32[lead:trail, :] = res_ref[:, lanes(h)].astype(jnp.float32)
        rows_f32[trail:, :] = jnp.where(seq == 0, edge, 0.0)
        group = 4

        @pl.loop(0, rows // group)
        def _(g):
            base = g * (group * width)
            for q in range(KERNEL):
                sums = [None] * group
                for r in range(group + KERNEL - 1):
                    start = pl.multiple_of(base + r * width, width)
                    line = rows_f32[pl.ds(start, width), :]
                    for o in range(group):
                        p = r - o
                        if 0 <= p < KERNEL:
                            term = line * taps[p, q : q + 1, lanes(h)]
                            sums[o] = term if sums[o] is None else sums[o] + term
                for o in range(group):
                    shifted[o, q, 8 : 8 + width, :] = sums[o]
            for o in range(group):
                value = shifted[o, margin, 8 : 8 + width, :] + vectors_ref[:, lanes(h)]
                for q in range(KERNEL):
                    if q != margin:
                        begin = 8 + q - margin
                        value = value + shifted[o, q, begin : begin + width, :]
                start = pl.multiple_of(base + o * width, width)
                acts[pl.ds(start, width), act_lanes(h, col)] = value.astype(jnp.bfloat16)

    def y_arrived(j):
        y_copy(j).wait_recv()
        core_copy(1, j).start()
        for part in far_x(j):
            part.start()

    def x_arrived(j):
        x_copy(j).wait_recv()
        for part in far_y(j):
            part.start()
        core_copy(2, j).start()

    def far_arrived(j):
        for part in far_y(j) + far_x(j):
            part.wait_recv()
        core_copy(3, j).start()

    @pl.loop(0, heads + lag)
    def _(h):
        @pl.when(h + ahead < heads)
        def _():
            key_copy(h + ahead).start()
            value_copy(h + ahead).start()

        for j, when in enumerate((2, 4, 6)):
            @pl.when(h == when)
            def _():
                x_copy(j).start()

        @pl.when(h < heads)
        def _():
            key_copy(h).wait_recv()
            value_copy(h).wait_recv()
            attend(h)
            halo_copy(h).start()

        @pl.when(h == heads)
        def _():
            for j in range(3, pieces):
                x_copy(j).start()

        @pl.when(h >= lag)
        def _():
            halo_copy(h - lag).wait_recv()
            convolve(h - lag)
            for i in range(planes - 1):
                act_copy(h - lag, i).start()

    res_copy.start()
    for j in range(5):
        y_arrived(j)
    x_arrived(0)
    y_arrived(5)
    x_arrived(1)
    y_arrived(6)
    x_arrived(2)
    y_arrived(7)
    x_arrived(3)
    x_arrived(4)

    @pl.loop(0, heads)
    def _(h):
        for i in range(planes - 1):
            act_arrival(h, i).wait_recv()
            act_copy(h, i).wait_send()

    block = 16
    inverse = 1.0 / acts.shape[1]

    @pl.loop(0, positions // block)
    def _(i):
        here = pl.ds(pl.multiple_of(i * block, block), block)
        wide = acts[here, :].astype(jnp.float32)
        center = jnp.sum(wide, axis=1, keepdims=True) * inverse
        wide = wide - center
        spread = jnp.sum(wide * wide, axis=1, keepdims=True) * inverse
        acts[here, :] = (
            wide * lax.rsqrt(spread + 1e-06) * vector(gain_at, channels) + vector(nbias_at, channels)
        ).astype(jnp.bfloat16)

    other = row + 1 - 2 * lax.rem(row, 2)
    places = []
    for r in (row, other):
        y = lax.rem(r + 2, 4)
        places.append([seq * 4 + r, seq * 4 + y, (1 - seq) * 4 + r, (1 - seq) * 4 + y])
    places = places[0] + places[1]

    def product(here, j, slots):
        result = None
        for slot in slots:
            cols = pl.ds(pl.multiple_of(places[slot] * depth, depth), depth)
            term = jnp.dot(
                acts[here, cols], weights[slot, j], preferred_element_type=jnp.float32
            )
            result = term if result is None else result + term
        return result

    tile = 256

    def first(j):
        @pl.loop(0, positions // tile)
        def _(i):
            here = pl.ds(pl.multiple_of(i * tile, tile), tile)
            total[j, here, :] = product(here, j, (0, 4, 1, 5))

    def second(j):
        core_copy(2, j).wait_recv()

        @pl.loop(0, positions // tile)
        def _(i):
            here = pl.ds(pl.multiple_of(i * tile, tile), tile)
            total[j, here, :] += product(here, j, (2, 6))

    def third(j):
        core_copy(3, j).wait_recv()
        cols = slice(j * piece, (j + 1) * piece)

        @pl.loop(0, positions // tile)
        def _(i):
            here = pl.ds(pl.multiple_of(i * tile, tile), tile)
            value = total[j, here, :] + product(here, j, (3, 7)) + vector(ebias_at + j * piece, piece)
            out_ref[here, cols] = (
                0.5 * value * (1.0 + lax.erf(value * (1.0 / math.sqrt(2.0))))
            ).astype(jnp.bfloat16)

        out_copy(j).start()

    for j in range(pieces):
        core_copy(0, j).wait_recv()
        core_copy(1, j).wait_recv()
    for j in range(4):
        first(j)
    x_arrived(5)
    far_arrived(0)
    for j in range(4, pieces):
        first(j)
    x_arrived(6)
    far_arrived(1)
    for j in range(4):
        second(j)
    far_arrived(2)
    x_arrived(7)
    for j in range(4, pieces):
        second(j)
    third(0)
    third(1)
    for j in range(3, pieces):
        far_arrived(j)
        third(j - 1)
    third(pieces - 1)
    res_copy.wait()

    @pl.loop(0, heads)
    def _(h):
        key_copy(h).wait_send()
        value_copy(h).wait_send()
        halo_copy(h).wait_send()

    for j in range(pieces):
        y_copy(j).wait_send()
        x_copy(j).wait_send()
        for part in far_y(j) + far_x(j):
            part.wait_send()
        out_copy(j).wait()
        for b in range(4):
            core_copy(b, j).wait_send()


def copy_out(res_in, out_in, res_ref, out_ref, res_held, out_held, load_sem, store_sem):
    loads, stores = [], []
    for i, (src, held, dst) in enumerate(
        ((out_in, out_held, out_ref), (res_in, res_held, res_ref))
    ):
        size = src.shape[0] // COPY_PARTS
        for n in range(COPY_PARTS):
            part = pl.ds(n * size, size)
            at = i * COPY_PARTS + n
            loads.append(pltpu.make_async_copy(src.at[part], held.at[part], load_sem.at[at]))
            stores.append(pltpu.make_async_copy(held.at[part], dst.at[part], store_sem.at[at]))
    for load in loads:
        load.start()
    for load, store in zip(loads, stores):
        load.wait()
        store.start()
    for store in stores:
        store.wait()


def on_device_kernel(
    planes,
    inputs,
    query_proj,
    key_proj,
    value_proj,
    depth_weight,
    depth_bias,
    norm_gain,
    norm_bias,
    expand_weight,
    expand_bias,
):
    _, rows, width, chans = inputs.shape
    positions, heads = rows * width, chans // HEAD_DIM
    depth, units = expand_weight.shape
    pieces = 8
    piece = units // pieces
    margin = KERNEL // 2

    def flat(array):
        return array.reshape(positions, chans)

    vectors = jnp.concatenate([depth_bias, norm_gain, norm_bias, expand_bias])
    vectors = lax.optimization_barrier(vectors.astype(jnp.float32)).reshape(1, -1)
    vmem, anywhere = pl.BlockSpec(memory_space=pltpu.VMEM), pl.BlockSpec(memory_space=pl.ANY)
    dma = pltpu.SemaphoreType.DMA
    residual, hidden = pl.pallas_call(
        functools.partial(whole_block, heads=heads, rows=rows, width=width, planes=planes),
        out_shape=(
            jax.ShapeDtypeStruct((positions, chans), jnp.bfloat16),
            jax.ShapeDtypeStruct((positions, units), jnp.bfloat16),
        ),
        in_specs=[anywhere] * 4 + [vmem] * 2 + [anywhere],
        out_specs=(anywhere, anywhere),
        scratch_shapes=[
            *[pltpu.VMEM((positions, chans), jnp.bfloat16)] * 5,
            pltpu.VMEM((positions, units), jnp.bfloat16),
            pltpu.VMEM((heads, positions, HEAD_DIM), jnp.bfloat16),
            pltpu.VMEM((heads, positions, HEAD_DIM), jnp.bfloat16),
            pltpu.VMEM((heads, margin * width, HEAD_DIM), jnp.bfloat16),
            pltpu.VMEM(((rows + 2 * margin) * width, HEAD_DIM), jnp.float32),
            pltpu.VMEM((4, KERNEL, width + 16, HEAD_DIM), jnp.float32),
            pltpu.VMEM((KERNEL, KERNEL, chans), jnp.float32),
            pltpu.VMEM((positions, planes * chans), jnp.bfloat16),
            pltpu.VMEM((8, pieces, depth, piece), jnp.bfloat16),
            pltpu.VMEM((pieces, positions, piece), jnp.float32),
            dma((4,)), dma((1,)), dma((pieces,)),
            dma((2 * heads,)), dma((2 * heads,)),
            dma((heads,)), dma((heads,)),
            dma(((planes - 1) * heads,)), dma(((planes - 1) * heads,)),
            dma((pieces,)),
            dma((pieces,)), dma((pieces,)),
            dma((pieces,)), dma((pieces,)),
            dma((pieces + 1,)), dma((pieces + 1,)),
            dma((4 * pieces,)), dma((4 * pieces,)),
        ],
        compiler_params=pltpu.CompilerParams(
            collective_id=0, has_side_effects=True, vmem_limit_bytes=VMEM_BYTES
        ),
    )(
        flat(inputs), flat(query_proj), flat(key_proj), flat(value_proj),
        depth_weight, vectors, expand_weight,
    )
    residual, hidden = pl.pallas_call(
        copy_out,
        out_shape=(
            jax.ShapeDtypeStruct((positions, chans), jnp.bfloat16),
            jax.ShapeDtypeStruct((positions, units), jnp.bfloat16),
        ),
        in_specs=[anywhere] * 2,
        out_specs=(anywhere, anywhere),
        scratch_shapes=[
            pltpu.VMEM((positions, chans), jnp.bfloat16),
            pltpu.VMEM((positions, units), jnp.bfloat16),
            dma((2 * COPY_PARTS,)),
            dma((2 * COPY_PARTS,)),
        ],
        compiler_params=pltpu.CompilerParams(vmem_limit_bytes=VMEM_BYTES),
    )(residual, hidden)
    return (residual.reshape(inputs.shape), hidden.reshape(1, rows, width, units))


def solution(mesh):
    body = on_device
    if mesh.shape["seq"] == 2 and mesh.shape["row"] == 4:
        body = functools.partial(on_device_kernel, mesh.shape["col"])
    return jax.shard_map(
        body,
        mesh=mesh,
        in_specs=(
            P("row", "seq", None, "col"),
            P("row", "seq", None, "col"),
            P("row", "seq", None, "col"),
            P("row", "seq", None, "col"),
            P(None, None, "col"),
            P("col"),
            P(),
            P(),
            P(("seq", "row"), "col"),
            P("col"),
        ),
        out_specs=(P("row", "seq", None, "col"), P("row", "seq", None, "col")),
        check_vma=False,
    )
```

```python
import functools
import math

import jax
import jax.numpy as jnp
from jax import lax
from jax.experimental import pallas as pl
from jax.experimental.pallas import tpu as pltpu
from jax.sharding import PartitionSpec as P

HEAD_DIM = 128
KERNEL = 7
COPY_PARTS = 8
VMEM_BYTES = 62 * 1024 * 1024


def padded_2(array, sides, width):
    for axis, dim in sides:
        peers, length = (lax.axis_size(axis), array.shape[dim])
        up = [(i, (i + 1) % peers) for i in range(peers - 1)]
        down = [(j, i) for i, j in up]
        last = lax.slice_in_dim(array, length - width, length, axis=dim)
        leading = lax.slice_in_dim(array, 0, width, axis=dim)
        before = lax.ppermute(last, axis, up)
        after = lax.ppermute(leading, axis, down)
        array = jnp.concatenate([before, array, after], axis=dim)
    return array


def on_device(
    inputs,
    query_proj,
    key_proj,
    value_proj,
    depth_weight,
    depth_bias,
    norm_gain,
    norm_bias,
    expand_weight,
    expand_bias,
):
    samples, rows_here, col_count, channels = inputs.shape
    heads_here = channels // HEAD_DIM
    positions = rows_here * col_count
    score_scale = 1.0 / math.sqrt(HEAD_DIM)
    queries = query_proj.reshape(samples, positions, heads_here, HEAD_DIM)
    start_max = jnp.full((samples, heads_here, positions), -1e30, jnp.float32)
    keys_in = lax.all_gather(key_proj, "seq", axis=1, tiled=True)
    values_in = lax.all_gather(value_proj, "seq", axis=1, tiled=True)
    count = keys_in.shape[1] * keys_in.shape[2]
    keys_in = keys_in.reshape(samples, count, heads_here, HEAD_DIM)
    values_in = values_in.reshape(samples, count, heads_here, HEAD_DIM)
    scores = (
        jnp.einsum("bqhd,bkhd->bhqk", queries, keys_in, preferred_element_type=jnp.float32)
        * score_scale
    )
    new_max = jnp.maximum(start_max, jnp.max(scores, axis=-1))
    weights = jnp.exp(scores - new_max[..., None])
    new_total = jnp.sum(weights, axis=-1)
    update = jnp.einsum(
        "bhqk,bkhd->bhqd",
        weights.astype(jnp.bfloat16),
        values_in,
        preferred_element_type=jnp.float32,
    )
    attended = update / new_total[..., None]
    attended = jnp.transpose(attended, (0, 2, 1, 3)).reshape(
        samples, rows_here, col_count, channels
    )
    residual_out = (inputs.astype(jnp.float32) + attended).astype(jnp.bfloat16)
    margin = KERNEL // 2
    padded = padded_2(residual_out, (("seq", 1),), margin)
    padded = jnp.pad(padded, ((0, 0), (0, 0), (margin, margin), (0, 0))).astype(jnp.float32)
    kernel_taps = depth_weight.astype(jnp.float32)
    convolved = jnp.zeros((samples, rows_here, col_count, channels), jnp.float32)
    for row_tap in range(KERNEL):
        for col_tap in range(KERNEL):
            convolved = (
                convolved
                + padded[:, row_tap : row_tap + rows_here, col_tap : col_tap + col_count, :]
                * kernel_taps[row_tap, col_tap]
            )
    convolved = (convolved + depth_bias.astype(jnp.float32)).astype(jnp.bfloat16)
    flat_rows = convolved.reshape(samples * positions, channels)
    gathered = lax.all_gather(flat_rows, "col", axis=1, tiled=True)
    widened = gathered.astype(jnp.float32)
    center = jnp.mean(widened, axis=1, keepdims=True)
    spread = jnp.mean((widened - center) * (widened - center), axis=1, keepdims=True)
    normed = (
        (widened - center) * lax.rsqrt(spread + 1e-06) * norm_gain.astype(jnp.float32)
        + norm_bias.astype(jnp.float32)
    ).astype(jnp.bfloat16)
    project = jnp.dot(
        normed,
        lax.all_gather(expand_weight, ("seq", "row"), axis=0, tiled=True),
        preferred_element_type=jnp.float32,
    )
    hidden = jax.nn.gelu(project + expand_bias.astype(jnp.float32), approximate=False).astype(
        jnp.bfloat16
    )
    return (residual_out, hidden.reshape(samples, rows_here, col_count, expand_weight.shape[1]))


def whole_block(
    x_hbm, q_hbm, k_hbm, v_hbm, taps_ref, vectors_ref, w_ref,
    res_hbm, out_hbm,
    x_ref, q_ref, k_ref, v_ref, res_ref, out_ref,
    k_in, v_in, halo, rows_f32, shifted, taps, acts, weights, total,
    in_sem, res_sem, out_sem, kv_send, kv_recv, halo_send, halo_recv, z_send, z_recv, own_sem,
    y_send, y_recv, x_send, x_recv, far_send, far_recv, core_send, core_recv,
    *, heads, rows, width, planes,
):
    seq, row, col = (lax.axis_index(a) for a in ("seq", "row", "col"))
    positions = rows * width
    margin = KERNEL // 2
    strip = margin * width
    chans = heads * HEAD_DIM
    depth = w_ref.shape[0]
    pieces, piece = total.shape[0], total.shape[2]
    by_y, ahead, lag = pieces * 3 // 4, 3, 2
    to_x = {"seq": 1 - seq}
    to_y = {"row": lax.rem(row + 2, 4)}
    to_core = {"row": row + 1 - 2 * lax.rem(row, 2)}
    z_peers = [{"col": lax.rem(col + i, planes)} for i in range(1, planes)]

    def remote(src, dst, send, recv, where):
        return pltpu.make_async_remote_copy(
            src_ref=src, dst_ref=dst, send_sem=send, recv_sem=recv,
            device_id=where, device_id_type=pl.DeviceIdType.MESH,
        )

    def lanes(h):
        return pl.ds(pl.multiple_of(h * HEAD_DIM, HEAD_DIM), HEAD_DIM)

    def key_copy(h):
        return remote(k_hbm.at[:, lanes(h)], k_in.at[h], kv_send.at[h], kv_recv.at[h], to_x)

    def value_copy(h):
        return remote(
            v_hbm.at[:, lanes(h)], v_in.at[h], kv_send.at[heads + h], kv_recv.at[heads + h], to_x
        )

    def halo_copy(h):
        start = pl.multiple_of((1 - seq) * (positions - strip), width)
        return remote(
            res_ref.at[pl.ds(start, strip), lanes(h)], halo.at[h],
            halo_send.at[h], halo_recv.at[h], to_x,
        )

    def act_lanes(h, plane):
        return pl.ds(pl.multiple_of(plane * chans + h * HEAD_DIM, HEAD_DIM), HEAD_DIM)

    def act_copy(h, i):
        part = acts.at[:, act_lanes(h, col)]
        return remote(
            part, part, z_send.at[i * heads + h], z_recv.at[i * heads + h], z_peers[i]
        )

    def act_arrival(h, i):
        plane = lax.rem(col + planes - i - 1, planes)
        part = acts.at[:, act_lanes(h, plane)]
        return remote(
            part, part, z_send.at[i * heads + h], z_recv.at[i * heads + h], z_peers[i]
        )

    def own_piece(j):
        return w_ref.at[:, pl.ds(j * piece, piece)]

    def own_copy(j):
        return pltpu.make_async_copy(own_piece(j), weights.at[0, j], own_sem.at[j])

    def y_copy(j):
        return remote(weights.at[0, j], weights.at[1, j], y_send.at[j], y_recv.at[j], to_y)

    def x_copy(j):
        return remote(weights.at[0, j], weights.at[2, j], x_send.at[j], x_recv.at[j], to_x)

    def far_part(j, rows_here, at, over_y):
        src, where = (2, to_y) if over_y else (1, to_x)
        return remote(
            weights.at[src, j, rows_here], weights.at[3, j, rows_here],
            far_send.at[at], far_recv.at[at], where,
        )

    def far_y(j):
        if j == by_y:
            return [far_part(j, pl.ds(0, depth // 2), j, True)]
        return [far_part(j, pl.ds(0, depth), j, True)] if j < by_y else []

    def far_x(j):
        if j >= pieces:
            return []
        if j == by_y:
            return [far_part(j, pl.ds(depth // 2, depth // 2), pieces, False)]
        return [far_part(j, pl.ds(0, depth), j, False)] if j > by_y else []

    def core_copy(b, j):
        at = b * pieces + j
        return remote(weights.at[b, j], weights.at[4 + b, j], core_send.at[at], core_recv.at[at], to_core)

    locals_in = [
        pltpu.make_async_copy(src, dst, in_sem.at[i])
        for i, (src, dst) in enumerate(
            ((q_hbm, q_ref), (k_hbm, k_ref), (v_hbm, v_ref), (x_hbm, x_ref))
        )
    ]
    res_copy = pltpu.make_async_copy(res_ref, res_hbm, res_sem.at[0])

    def out_copy(j):
        part = (slice(None), pl.ds(j * piece, piece))
        return pltpu.make_async_copy(out_ref.at[part], out_hbm.at[part], out_sem.at[j])

    for copy in locals_in:
        copy.start()
    for j in range(pieces):
        own_copy(j).start()
    barrier = pltpu.get_barrier_semaphore()
    peers = [to_x, to_y, to_core] + z_peers
    for peer in peers:
        pl.semaphore_signal(
            barrier, inc=1, device_id=peer, device_id_type=pl.DeviceIdType.MESH
        )
    pl.semaphore_wait(barrier, len(peers))

    for h in range(min(ahead, heads)):
        key_copy(h).start()
        value_copy(h).start()
    for j in range(pieces):
        own_copy(j).wait()
        y_copy(j).start()
        core_copy(0, j).start()

    scale = 1.0 / math.sqrt(HEAD_DIM)
    half = positions // 2
    shifted[...] = jnp.zeros_like(shifted)
    taps[...] = taps_ref[...].astype(jnp.float32)

    for copy in locals_in:
        copy.wait()
    channels = acts.shape[1]
    gain_at, nbias_at = chans, chans + channels
    ebias_at = nbias_at + channels

    def vector(start, size):
        return vectors_ref[:, pl.ds(start, size)]

    def attend(h):
        keys, values = k_ref[:, lanes(h)], v_ref[:, lanes(h)]
        far_keys, far_values = k_in[h], v_in[h]
        over = (((1,), (1,)), ((), ()))

        @pl.loop(0, 2)
        def _(i):
            here = pl.ds(pl.multiple_of(i * half, half), half)
            queries = q_ref[here, lanes(h)]
            near = lax.dot_general(queries, keys, over, preferred_element_type=jnp.float32) * scale
            far = lax.dot_general(queries, far_keys, over, preferred_element_type=jnp.float32) * scale
            peak = jnp.maximum(
                jnp.max(near, axis=1, keepdims=True), jnp.max(far, axis=1, keepdims=True)
            )
            near, far = jnp.exp(near - peak), jnp.exp(far - peak)
            count = jnp.sum(near, axis=1, keepdims=True) + jnp.sum(far, axis=1, keepdims=True)
            mixed = jnp.dot(
                near.astype(jnp.bfloat16), values, preferred_element_type=jnp.float32
            ) + jnp.dot(far.astype(jnp.bfloat16), far_values, preferred_element_type=jnp.float32)
            res_ref[here, lanes(h)] = (
                x_ref[here, lanes(h)].astype(jnp.float32) + mixed / count
            ).astype(jnp.bfloat16)

    def convolve(h):
        edge = halo[h].astype(jnp.float32)
        lead, trail = margin * width, (margin + rows) * width
        rows_f32[0:lead, :] = jnp.where(seq == 1, edge, 0.0)
        rows_f32[lead:trail, :] = res_ref[:, lanes(h)].astype(jnp.float32)
        rows_f32[trail:, :] = jnp.where(seq == 0, edge, 0.0)
        group = 4

        @pl.loop(0, rows // group)
        def _(g):
            base = g * (group * width)
            for q in range(KERNEL):
                sums = [None] * group
                for r in range(group + KERNEL - 1):
                    start = pl.multiple_of(base + r * width, width)
                    line = rows_f32[pl.ds(start, width), :]
                    for o in range(group):
                        p = r - o
                        if 0 <= p < KERNEL:
                            term = line * taps[p, q : q + 1, lanes(h)]
                            sums[o] = term if sums[o] is None else sums[o] + term
                for o in range(group):
                    shifted[o, q, 8 : 8 + width, :] = sums[o]
            for o in range(group):
                value = shifted[o, margin, 8 : 8 + width, :] + vectors_ref[:, lanes(h)]
                for q in range(KERNEL):
                    if q != margin:
                        begin = 8 + q - margin
                        value = value + shifted[o, q, begin : begin + width, :]
                start = pl.multiple_of(base + o * width, width)
                acts[pl.ds(start, width), act_lanes(h, col)] = value.astype(jnp.bfloat16)

    def y_arrived(j):
        y_copy(j).wait_recv()
        core_copy(1, j).start()

    def x_arrived(j):
        x_copy(j).wait_recv()
        for part in far_y(j):
            part.start()
        if 5 <= j + 3 < pieces:
            x_copy(j + 3).start()
        for part in far_x(j + 1):
            part.start()
        core_copy(2, j).start()

    def far_arrived(j):
        for part in far_y(j) + far_x(j):
            part.wait_recv()
        core_copy(3, j).start()

    @pl.loop(0, heads + lag)
    def _(h):
        @pl.when(h + ahead < heads)
        def _():
            key_copy(h + ahead).start()
            value_copy(h + ahead).start()

        for j, when in enumerate((2, 4, 6)):
            @pl.when(h == when)
            def _():
                x_copy(j).start()

        @pl.when(h < heads)
        def _():
            key_copy(h).wait_recv()
            value_copy(h).wait_recv()
            attend(h)
            halo_copy(h).start()

        @pl.when(h == heads)
        def _():
            for j in range(3, 5):
                x_copy(j).start()

        @pl.when(h >= lag)
        def _():
            halo_copy(h - lag).wait_recv()
            convolve(h - lag)
            for i in range(planes - 1):
                act_copy(h - lag, i).start()

    res_copy.start()
    for j in range(5):
        y_arrived(j)
    x_arrived(0)
    y_arrived(5)
    x_arrived(1)
    y_arrived(6)
    x_arrived(2)
    y_arrived(7)
    x_arrived(3)
    x_arrived(4)

    @pl.loop(0, heads)
    def _(h):
        for i in range(planes - 1):
            act_arrival(h, i).wait_recv()
            act_copy(h, i).wait_send()

    block = 16
    inverse = 1.0 / acts.shape[1]

    @pl.loop(0, positions // block)
    def _(i):
        here = pl.ds(pl.multiple_of(i * block, block), block)
        wide = acts[here, :].astype(jnp.float32)
        center = jnp.sum(wide, axis=1, keepdims=True) * inverse
        wide = wide - center
        spread = jnp.sum(wide * wide, axis=1, keepdims=True) * inverse
        acts[here, :] = (
            wide * lax.rsqrt(spread + 1e-06) * vector(gain_at, channels) + vector(nbias_at, channels)
        ).astype(jnp.bfloat16)

    other = row + 1 - 2 * lax.rem(row, 2)
    places = []
    for r in (row, other):
        y = lax.rem(r + 2, 4)
        places.append([seq * 4 + r, seq * 4 + y, (1 - seq) * 4 + r, (1 - seq) * 4 + y])
    places = places[0] + places[1]

    tile = min(256, piece)

    def product(here, j, slots):
        result = None
        for slot in slots:
            cols = pl.ds(pl.multiple_of(places[slot] * depth, depth), depth)
            term = jnp.dot(
                acts[:, cols], weights[slot, j, :, here], preferred_element_type=jnp.float32
            )
            result = term if result is None else result + term
        return result

    def first(j):
        @pl.loop(0, piece // tile)
        def _(i):
            here = pl.ds(pl.multiple_of(i * tile, tile), tile)
            total[j, :, here] = product(here, j, (0, 4, 1, 5))

    def second(j):
        core_copy(2, j).wait_recv()

        @pl.loop(0, piece // tile)
        def _(i):
            here = pl.ds(pl.multiple_of(i * tile, tile), tile)
            total[j, :, here] += product(here, j, (2, 6))

    def third(j):
        core_copy(3, j).wait_recv()

        @pl.loop(0, piece // tile)
        def _(i):
            here = pl.ds(pl.multiple_of(i * tile, tile), tile)
            cols = pl.ds(pl.multiple_of(j * piece + i * tile, tile), tile)
            bias = pl.ds(pl.multiple_of(ebias_at + j * piece + i * tile, tile), tile)
            value = total[j, :, here] + product(here, j, (3, 7)) + vectors_ref[:, bias]
            out_ref[:, cols] = (
                0.5 * value * (1.0 + lax.erf(value * (1.0 / math.sqrt(2.0))))
            ).astype(jnp.bfloat16)

        out_copy(j).start()

    for j in range(pieces):
        core_copy(0, j).wait_recv()
        core_copy(1, j).wait_recv()
    x_arrived(5)
    for j in range(4):
        first(j)
    far_arrived(0)
    x_arrived(6)
    for j in range(4, pieces):
        first(j)
    far_arrived(1)
    for j in range(4):
        second(j)
    far_arrived(2)
    x_arrived(7)
    for j in range(4, pieces):
        second(j)
    third(0)
    third(1)
    for j in range(3, pieces):
        far_arrived(j)
        third(j - 1)
    third(pieces - 1)
    res_copy.wait()

    @pl.loop(0, heads)
    def _(h):
        key_copy(h).wait_send()
        value_copy(h).wait_send()
        halo_copy(h).wait_send()

    for j in range(pieces):
        y_copy(j).wait_send()
        x_copy(j).wait_send()
        for part in far_y(j) + far_x(j):
            part.wait_send()
        out_copy(j).wait()
        for b in range(4):
            core_copy(b, j).wait_send()


def copy_out(res_in, out_in, res_ref, out_ref, res_held, out_held, load_sem, store_sem):
    loads, stores = [], []
    for i, (src, held, dst) in enumerate(
        ((out_in, out_held, out_ref), (res_in, res_held, res_ref))
    ):
        size = src.shape[0] // COPY_PARTS
        for n in range(COPY_PARTS):
            part = pl.ds(n * size, size)
            at = i * COPY_PARTS + n
            loads.append(pltpu.make_async_copy(src.at[part], held.at[part], load_sem.at[at]))
            stores.append(pltpu.make_async_copy(held.at[part], dst.at[part], store_sem.at[at]))
    for load in loads:
        load.start()
    for load, store in zip(loads, stores):
        load.wait()
        store.start()
    for store in stores:
        store.wait()


def on_device_kernel(
    planes,
    inputs,
    query_proj,
    key_proj,
    value_proj,
    depth_weight,
    depth_bias,
    norm_gain,
    norm_bias,
    expand_weight,
    expand_bias,
):
    _, rows, width, chans = inputs.shape
    positions, heads = rows * width, chans // HEAD_DIM
    depth, units = expand_weight.shape
    pieces = 8
    piece = units // pieces
    margin = KERNEL // 2

    def flat(array):
        return array.reshape(positions, chans)

    vectors = jnp.concatenate([depth_bias, norm_gain, norm_bias, expand_bias])
    vectors = lax.optimization_barrier(vectors.astype(jnp.float32)).reshape(1, -1)
    vmem, anywhere = pl.BlockSpec(memory_space=pltpu.VMEM), pl.BlockSpec(memory_space=pl.ANY)
    dma = pltpu.SemaphoreType.DMA
    residual, hidden = pl.pallas_call(
        functools.partial(whole_block, heads=heads, rows=rows, width=width, planes=planes),
        out_shape=(
            jax.ShapeDtypeStruct((positions, chans), jnp.bfloat16),
            jax.ShapeDtypeStruct((positions, units), jnp.bfloat16),
        ),
        in_specs=[anywhere] * 4 + [vmem] * 2 + [anywhere],
        out_specs=(anywhere, anywhere),
        scratch_shapes=[
            *[pltpu.VMEM((positions, chans), jnp.bfloat16)] * 5,
            pltpu.VMEM((positions, units), jnp.bfloat16),
            pltpu.VMEM((heads, positions, HEAD_DIM), jnp.bfloat16),
            pltpu.VMEM((heads, positions, HEAD_DIM), jnp.bfloat16),
            pltpu.VMEM((heads, margin * width, HEAD_DIM), jnp.bfloat16),
            pltpu.VMEM(((rows + 2 * margin) * width, HEAD_DIM), jnp.float32),
            pltpu.VMEM((4, KERNEL, width + 16, HEAD_DIM), jnp.float32),
            pltpu.VMEM((KERNEL, KERNEL, chans), jnp.float32),
            pltpu.VMEM((positions, planes * chans), jnp.bfloat16),
            pltpu.VMEM((8, pieces, depth, piece), jnp.bfloat16),
            pltpu.VMEM((pieces, positions, piece), jnp.float32),
            dma((4,)), dma((1,)), dma((pieces,)),
            dma((2 * heads,)), dma((2 * heads,)),
            dma((heads,)), dma((heads,)),
            dma(((planes - 1) * heads,)), dma(((planes - 1) * heads,)),
            dma((pieces,)),
            dma((pieces,)), dma((pieces,)),
            dma((pieces,)), dma((pieces,)),
            dma((pieces + 1,)), dma((pieces + 1,)),
            dma((4 * pieces,)), dma((4 * pieces,)),
        ],
        compiler_params=pltpu.CompilerParams(
            collective_id=0, has_side_effects=True, vmem_limit_bytes=VMEM_BYTES
        ),
    )(
        flat(inputs), flat(query_proj), flat(key_proj), flat(value_proj),
        depth_weight, vectors, expand_weight,
    )
    residual, hidden = pl.pallas_call(
        copy_out,
        out_shape=(
            jax.ShapeDtypeStruct((positions, chans), jnp.bfloat16),
            jax.ShapeDtypeStruct((positions, units), jnp.bfloat16),
        ),
        in_specs=[anywhere] * 2,
        out_specs=(anywhere, anywhere),
        scratch_shapes=[
            pltpu.VMEM((positions, chans), jnp.bfloat16),
            pltpu.VMEM((positions, units), jnp.bfloat16),
            dma((2 * COPY_PARTS,)),
            dma((2 * COPY_PARTS,)),
        ],
        compiler_params=pltpu.CompilerParams(vmem_limit_bytes=VMEM_BYTES),
    )(residual, hidden)
    return (residual.reshape(inputs.shape), hidden.reshape(1, rows, width, units))


def solution(mesh):
    body = on_device
    if mesh.shape["seq"] == 2 and mesh.shape["row"] == 4:
        body = functools.partial(on_device_kernel, mesh.shape["col"])
    return jax.shard_map(
        body,
        mesh=mesh,
        in_specs=(
            P("row", "seq", None, "col"),
            P("row", "seq", None, "col"),
            P("row", "seq", None, "col"),
            P("row", "seq", None, "col"),
            P(None, None, "col"),
            P("col"),
            P(),
            P(),
            P(("seq", "row"), "col"),
            P("col"),
        ),
        out_specs=(P("row", "seq", None, "col"), P("row", "seq", None, "col")),
        check_vma=False,
    )
```

```python
import functools
import math

import jax
import jax.numpy as jnp
from jax import lax
from jax.experimental import pallas as pl
from jax.experimental.pallas import tpu as pltpu
from jax.sharding import PartitionSpec as P

HEAD_DIM = 128
KERNEL = 7
COPY_PARTS = 8
VMEM_BYTES = 62 * 1024 * 1024


def padded_2(array, sides, width):
    for axis, dim in sides:
        peers, length = (lax.axis_size(axis), array.shape[dim])
        up = [(i, (i + 1) % peers) for i in range(peers - 1)]
        down = [(j, i) for i, j in up]
        last = lax.slice_in_dim(array, length - width, length, axis=dim)
        leading = lax.slice_in_dim(array, 0, width, axis=dim)
        before = lax.ppermute(last, axis, up)
        after = lax.ppermute(leading, axis, down)
        array = jnp.concatenate([before, array, after], axis=dim)
    return array


def on_device(
    inputs,
    query_proj,
    key_proj,
    value_proj,
    depth_weight,
    depth_bias,
    norm_gain,
    norm_bias,
    expand_weight,
    expand_bias,
):
    samples, rows_here, col_count, channels = inputs.shape
    heads_here = channels // HEAD_DIM
    positions = rows_here * col_count
    score_scale = 1.0 / math.sqrt(HEAD_DIM)
    queries = query_proj.reshape(samples, positions, heads_here, HEAD_DIM)
    start_max = jnp.full((samples, heads_here, positions), -1e30, jnp.float32)
    keys_in = lax.all_gather(key_proj, "seq", axis=1, tiled=True)
    values_in = lax.all_gather(value_proj, "seq", axis=1, tiled=True)
    count = keys_in.shape[1] * keys_in.shape[2]
    keys_in = keys_in.reshape(samples, count, heads_here, HEAD_DIM)
    values_in = values_in.reshape(samples, count, heads_here, HEAD_DIM)
    scores = (
        jnp.einsum("bqhd,bkhd->bhqk", queries, keys_in, preferred_element_type=jnp.float32)
        * score_scale
    )
    new_max = jnp.maximum(start_max, jnp.max(scores, axis=-1))
    weights = jnp.exp(scores - new_max[..., None])
    new_total = jnp.sum(weights, axis=-1)
    update = jnp.einsum(
        "bhqk,bkhd->bhqd",
        weights.astype(jnp.bfloat16),
        values_in,
        preferred_element_type=jnp.float32,
    )
    attended = update / new_total[..., None]
    attended = jnp.transpose(attended, (0, 2, 1, 3)).reshape(
        samples, rows_here, col_count, channels
    )
    residual_out = (inputs.astype(jnp.float32) + attended).astype(jnp.bfloat16)
    margin = KERNEL // 2
    padded = padded_2(residual_out, (("seq", 1),), margin)
    padded = jnp.pad(padded, ((0, 0), (0, 0), (margin, margin), (0, 0))).astype(jnp.float32)
    kernel_taps = depth_weight.astype(jnp.float32)
    convolved = jnp.zeros((samples, rows_here, col_count, channels), jnp.float32)
    for row_tap in range(KERNEL):
        for col_tap in range(KERNEL):
            convolved = (
                convolved
                + padded[:, row_tap : row_tap + rows_here, col_tap : col_tap + col_count, :]
                * kernel_taps[row_tap, col_tap]
            )
    convolved = (convolved + depth_bias.astype(jnp.float32)).astype(jnp.bfloat16)
    flat_rows = convolved.reshape(samples * positions, channels)
    gathered = lax.all_gather(flat_rows, "col", axis=1, tiled=True)
    widened = gathered.astype(jnp.float32)
    center = jnp.mean(widened, axis=1, keepdims=True)
    spread = jnp.mean((widened - center) * (widened - center), axis=1, keepdims=True)
    normed = (
        (widened - center) * lax.rsqrt(spread + 1e-06) * norm_gain.astype(jnp.float32)
        + norm_bias.astype(jnp.float32)
    ).astype(jnp.bfloat16)
    project = jnp.dot(
        normed,
        lax.all_gather(expand_weight, ("seq", "row"), axis=0, tiled=True),
        preferred_element_type=jnp.float32,
    )
    hidden = jax.nn.gelu(project + expand_bias.astype(jnp.float32), approximate=False).astype(
        jnp.bfloat16
    )
    return (residual_out, hidden.reshape(samples, rows_here, col_count, expand_weight.shape[1]))


def whole_block(
    x_hbm, q_hbm, k_hbm, v_hbm, taps_ref, vectors_ref, w_ref,
    res_hbm, out_hbm,
    x_ref, q_ref, k_ref, v_ref, res_ref, out_ref,
    k_in, v_in, halo, rows_f32, shifted, taps, acts, weights, total,
    in_sem, res_sem, out_sem, kv_send, kv_recv, halo_send, halo_recv, z_send, z_recv, own_sem,
    y_send, y_recv, x_send, x_recv, far_send, far_recv, core_send, core_recv,
    *, heads, rows, width, planes,
):
    seq, row, col = (lax.axis_index(a) for a in ("seq", "row", "col"))
    positions = rows * width
    margin = KERNEL // 2
    strip = margin * width
    chans = heads * HEAD_DIM
    depth = w_ref.shape[0]
    pieces, piece = total.shape[0], total.shape[2]
    by_y, ahead, lag = pieces * 3 // 4, 3, 2
    to_x = {"seq": 1 - seq}
    to_y = {"row": lax.rem(row + 2, 4)}
    to_core = {"row": row + 1 - 2 * lax.rem(row, 2)}
    z_peers = [{"col": lax.rem(col + i, planes)} for i in range(1, planes)]

    def remote(src, dst, send, recv, where):
        return pltpu.make_async_remote_copy(
            src_ref=src, dst_ref=dst, send_sem=send, recv_sem=recv,
            device_id=where, device_id_type=pl.DeviceIdType.MESH,
        )

    def lanes(h):
        return pl.ds(pl.multiple_of(h * HEAD_DIM, HEAD_DIM), HEAD_DIM)

    def key_copy(h):
        return remote(k_hbm.at[:, lanes(h)], k_in.at[h], kv_send.at[h], kv_recv.at[h], to_x)

    def value_copy(h):
        return remote(
            v_hbm.at[:, lanes(h)], v_in.at[h], kv_send.at[heads + h], kv_recv.at[heads + h], to_x
        )

    def halo_copy(h):
        start = pl.multiple_of((1 - seq) * (positions - strip), width)
        return remote(
            res_ref.at[pl.ds(start, strip), lanes(h)], halo.at[h],
            halo_send.at[h], halo_recv.at[h], to_x,
        )

    def act_lanes(h, plane):
        return pl.ds(pl.multiple_of(plane * chans + h * HEAD_DIM, HEAD_DIM), HEAD_DIM)

    def act_copy(h, i):
        part = acts.at[:, act_lanes(h, col)]
        return remote(
            part, part, z_send.at[i * heads + h], z_recv.at[i * heads + h], z_peers[i]
        )

    def act_arrival(h, i):
        plane = lax.rem(col + planes - i - 1, planes)
        part = acts.at[:, act_lanes(h, plane)]
        return remote(
            part, part, z_send.at[i * heads + h], z_recv.at[i * heads + h], z_peers[i]
        )

    def own_piece(j):
        return w_ref.at[:, pl.ds(j * piece, piece)]

    def own_copy(j):
        return pltpu.make_async_copy(own_piece(j), weights.at[0, j], own_sem.at[j])

    def y_copy(j):
        return remote(weights.at[0, j], weights.at[1, j], y_send.at[j], y_recv.at[j], to_y)

    def x_copy(j):
        return remote(weights.at[0, j], weights.at[2, j], x_send.at[j], x_recv.at[j], to_x)

    def far_part(j, rows_here, at, over_y):
        src, where = (2, to_y) if over_y else (1, to_x)
        return remote(
            weights.at[src, j, rows_here], weights.at[3, j, rows_here],
            far_send.at[at], far_recv.at[at], where,
        )

    def far_y(j):
        if j == by_y:
            return [far_part(j, pl.ds(0, depth // 2), j, True)]
        return [far_part(j, pl.ds(0, depth), j, True)] if j < by_y else []

    def far_x(j):
        if j >= pieces:
            return []
        if j == by_y:
            return [far_part(j, pl.ds(depth // 2, depth // 2), pieces, False)]
        return [far_part(j, pl.ds(0, depth), j, False)] if j > by_y else []

    def core_copy(b, j):
        at = b * pieces + j
        return remote(weights.at[b, j], weights.at[4 + b, j], core_send.at[at], core_recv.at[at], to_core)

    locals_in = [
        pltpu.make_async_copy(src, dst, in_sem.at[i])
        for i, (src, dst) in enumerate(
            ((q_hbm, q_ref), (k_hbm, k_ref), (v_hbm, v_ref), (x_hbm, x_ref))
        )
    ]
    res_copy = pltpu.make_async_copy(res_ref, res_hbm, res_sem.at[0])

    def out_copy(j):
        part = (slice(None), pl.ds(j * piece, piece))
        return pltpu.make_async_copy(out_ref.at[part], out_hbm.at[part], out_sem.at[j])

    for copy in locals_in:
        copy.start()
    for j in range(pieces):
        own_copy(j).start()
    barrier = pltpu.get_barrier_semaphore()
    peers = [to_x, to_y, to_core] + z_peers
    for peer in peers:
        pl.semaphore_signal(
            barrier, inc=1, device_id=peer, device_id_type=pl.DeviceIdType.MESH
        )
    pl.semaphore_wait(barrier, len(peers))

    for h in range(min(ahead, heads)):
        key_copy(h).start()
        value_copy(h).start()
    for j in range(pieces):
        own_copy(j).wait()
        y_copy(j).start()
        core_copy(0, j).start()

    scale = 1.0 / math.sqrt(HEAD_DIM)
    half = positions // 2
    shifted[...] = jnp.zeros_like(shifted)
    taps[...] = taps_ref[...].astype(jnp.float32)

    for copy in locals_in:
        copy.wait()
    channels = acts.shape[1]
    gain_at, nbias_at = chans, chans + channels
    ebias_at = nbias_at + channels

    def vector(start, size):
        return vectors_ref[:, pl.ds(start, size)]

    def attend(h):
        keys, values = k_ref[:, lanes(h)], v_ref[:, lanes(h)]
        far_keys, far_values = k_in[h], v_in[h]
        over = (((1,), (1,)), ((), ()))

        @pl.loop(0, 2)
        def _(i):
            here = pl.ds(pl.multiple_of(i * half, half), half)
            queries = q_ref[here, lanes(h)]
            near = lax.dot_general(queries, keys, over, preferred_element_type=jnp.float32) * scale
            far = lax.dot_general(queries, far_keys, over, preferred_element_type=jnp.float32) * scale
            peak = jnp.maximum(
                jnp.max(near, axis=1, keepdims=True), jnp.max(far, axis=1, keepdims=True)
            )
            near, far = jnp.exp(near - peak), jnp.exp(far - peak)
            count = jnp.sum(near, axis=1, keepdims=True) + jnp.sum(far, axis=1, keepdims=True)
            mixed = jnp.dot(
                near.astype(jnp.bfloat16), values, preferred_element_type=jnp.float32
            ) + jnp.dot(far.astype(jnp.bfloat16), far_values, preferred_element_type=jnp.float32)
            res_ref[here, lanes(h)] = (
                x_ref[here, lanes(h)].astype(jnp.float32) + mixed / count
            ).astype(jnp.bfloat16)

    def convolve(h):
        edge = halo[h].astype(jnp.float32)
        lead, trail = margin * width, (margin + rows) * width
        rows_f32[0:lead, :] = jnp.where(seq == 1, edge, 0.0)
        rows_f32[lead:trail, :] = res_ref[:, lanes(h)].astype(jnp.float32)
        rows_f32[trail:, :] = jnp.where(seq == 0, edge, 0.0)
        group = 4

        @pl.loop(0, rows // group)
        def _(g):
            base = g * (group * width)
            for q in range(KERNEL):
                sums = [None] * group
                for r in range(group + KERNEL - 1):
                    start = pl.multiple_of(base + r * width, width)
                    line = rows_f32[pl.ds(start, width), :]
                    for o in range(group):
                        p = r - o
                        if 0 <= p < KERNEL:
                            term = line * taps[p, q : q + 1, lanes(h)]
                            sums[o] = term if sums[o] is None else sums[o] + term
                for o in range(group):
                    shifted[o, q, 8 : 8 + width, :] = sums[o]
            for o in range(group):
                value = shifted[o, margin, 8 : 8 + width, :] + vectors_ref[:, lanes(h)]
                for q in range(KERNEL):
                    if q != margin:
                        begin = 8 + q - margin
                        value = value + shifted[o, q, begin : begin + width, :]
                start = pl.multiple_of(base + o * width, width)
                acts[pl.ds(start, width), act_lanes(h, col)] = value.astype(jnp.bfloat16)

    def y_arrived(j):
        y_copy(j).wait_recv()
        core_copy(1, j).start()

    def x_arrived(j):
        x_copy(j).wait_recv()
        for part in far_y(j):
            part.start()
        for part in far_x(j + 1):
            part.start()
        core_copy(2, j).start()

    def far_arrived(j):
        for part in far_y(j) + far_x(j):
            part.wait_recv()
        core_copy(3, j).start()

    @pl.loop(0, heads + lag)
    def _(h):
        @pl.when(h + ahead < heads)
        def _():
            key_copy(h + ahead).start()
            value_copy(h + ahead).start()

        for j, when in enumerate((1, 2, 4, 5, 6, 7)):
            @pl.when(h == when)
            def _():
                x_copy(j).start()

        @pl.when(h < heads)
        def _():
            key_copy(h).wait_recv()
            value_copy(h).wait_recv()
            attend(h)
            halo_copy(h).start()

        @pl.when(h == heads)
        def _():
            for j in range(6, pieces):
                x_copy(j).start()

        for j in range(3):
            @pl.when(h == heads - 1 + j)
            def _():
                x_arrived(j)

        @pl.when(h >= lag)
        def _():
            halo_copy(h - lag).wait_recv()
            convolve(h - lag)
            for i in range(planes - 1):
                act_copy(h - lag, i).start()

    res_copy.start()
    for j in range(5):
        y_arrived(j)
    for j in range(5, pieces):
        y_arrived(j)
    x_arrived(3)
    x_arrived(4)

    @pl.loop(0, heads)
    def _(h):
        for i in range(planes - 1):
            act_arrival(h, i).wait_recv()
            act_copy(h, i).wait_send()

    block = 16
    inverse = 1.0 / acts.shape[1]

    @pl.loop(0, positions // block)
    def _(i):
        here = pl.ds(pl.multiple_of(i * block, block), block)
        wide = acts[here, :].astype(jnp.float32)
        center = jnp.sum(wide, axis=1, keepdims=True) * inverse
        wide = wide - center
        spread = jnp.sum(wide * wide, axis=1, keepdims=True) * inverse
        acts[here, :] = (
            wide * lax.rsqrt(spread + 1e-06) * vector(gain_at, channels) + vector(nbias_at, channels)
        ).astype(jnp.bfloat16)

    other = row + 1 - 2 * lax.rem(row, 2)
    places = []
    for r in (row, other):
        y = lax.rem(r + 2, 4)
        places.append([seq * 4 + r, seq * 4 + y, (1 - seq) * 4 + r, (1 - seq) * 4 + y])
    places = places[0] + places[1]

    tile = min(256, piece)

    def product(here, j, slots):
        result = None
        for slot in slots:
            cols = pl.ds(pl.multiple_of(places[slot] * depth, depth), depth)
            term = jnp.dot(
                acts[:, cols], weights[slot, j, :, here], preferred_element_type=jnp.float32
            )
            result = term if result is None else result + term
        return result

    def first(j):
        @pl.loop(0, piece // tile)
        def _(i):
            here = pl.ds(pl.multiple_of(i * tile, tile), tile)
            total[j, :, here] = product(here, j, (0, 4, 1, 5))

    def second(j):
        core_copy(2, j).wait_recv()

        @pl.loop(0, piece // tile)
        def _(i):
            here = pl.ds(pl.multiple_of(i * tile, tile), tile)
            total[j, :, here] += product(here, j, (2, 6))

    def third(j):
        core_copy(3, j).wait_recv()

        @pl.loop(0, piece // tile)
        def _(i):
            here = pl.ds(pl.multiple_of(i * tile, tile), tile)
            cols = pl.ds(pl.multiple_of(j * piece + i * tile, tile), tile)
            bias = pl.ds(pl.multiple_of(ebias_at + j * piece + i * tile, tile), tile)
            value = total[j, :, here] + product(here, j, (3, 7)) + vectors_ref[:, bias]
            out_ref[:, cols] = (
                0.5 * value * (1.0 + lax.erf(value * (1.0 / math.sqrt(2.0))))
            ).astype(jnp.bfloat16)

        out_copy(j).start()

    for j in range(pieces):
        core_copy(0, j).wait_recv()
        core_copy(1, j).wait_recv()
    x_arrived(5)
    for j in range(4):
        first(j)
    far_arrived(0)
    x_arrived(6)
    for j in range(4, pieces):
        first(j)
    far_arrived(1)
    for j in range(4):
        second(j)
    far_arrived(2)
    x_arrived(7)
    for j in range(4, pieces):
        second(j)
    third(0)
    third(1)
    for j in range(3, pieces):
        far_arrived(j)
        third(j - 1)
    third(pieces - 1)
    res_copy.wait()

    @pl.loop(0, heads)
    def _(h):
        key_copy(h).wait_send()
        value_copy(h).wait_send()
        halo_copy(h).wait_send()

    for j in range(pieces):
        y_copy(j).wait_send()
        x_copy(j).wait_send()
        for part in far_y(j) + far_x(j):
            part.wait_send()
        out_copy(j).wait()
        for b in range(4):
            core_copy(b, j).wait_send()


def copy_out(res_in, out_in, res_ref, out_ref, res_held, out_held, load_sem, store_sem):
    loads, stores = [], []
    for i, (src, held, dst) in enumerate(
        ((out_in, out_held, out_ref), (res_in, res_held, res_ref))
    ):
        size = src.shape[0] // COPY_PARTS
        for n in range(COPY_PARTS):
            part = pl.ds(n * size, size)
            at = i * COPY_PARTS + n
            loads.append(pltpu.make_async_copy(src.at[part], held.at[part], load_sem.at[at]))
            stores.append(pltpu.make_async_copy(held.at[part], dst.at[part], store_sem.at[at]))
    for load in loads:
        load.start()
    for load, store in zip(loads, stores):
        load.wait()
        store.start()
    for store in stores:
        store.wait()


def on_device_kernel(
    planes,
    inputs,
    query_proj,
    key_proj,
    value_proj,
    depth_weight,
    depth_bias,
    norm_gain,
    norm_bias,
    expand_weight,
    expand_bias,
):
    _, rows, width, chans = inputs.shape
    positions, heads = rows * width, chans // HEAD_DIM
    depth, units = expand_weight.shape
    pieces = 8
    piece = units // pieces
    margin = KERNEL // 2

    def flat(array):
        return array.reshape(positions, chans)

    vectors = jnp.concatenate([depth_bias, norm_gain, norm_bias, expand_bias])
    vectors = lax.optimization_barrier(vectors.astype(jnp.float32)).reshape(1, -1)
    vmem, anywhere = pl.BlockSpec(memory_space=pltpu.VMEM), pl.BlockSpec(memory_space=pl.ANY)
    dma = pltpu.SemaphoreType.DMA
    residual, hidden = pl.pallas_call(
        functools.partial(whole_block, heads=heads, rows=rows, width=width, planes=planes),
        out_shape=(
            jax.ShapeDtypeStruct((positions, chans), jnp.bfloat16),
            jax.ShapeDtypeStruct((positions, units), jnp.bfloat16),
        ),
        in_specs=[anywhere] * 4 + [vmem] * 2 + [anywhere],
        out_specs=(anywhere, anywhere),
        scratch_shapes=[
            *[pltpu.VMEM((positions, chans), jnp.bfloat16)] * 5,
            pltpu.VMEM((positions, units), jnp.bfloat16),
            pltpu.VMEM((heads, positions, HEAD_DIM), jnp.bfloat16),
            pltpu.VMEM((heads, positions, HEAD_DIM), jnp.bfloat16),
            pltpu.VMEM((heads, margin * width, HEAD_DIM), jnp.bfloat16),
            pltpu.VMEM(((rows + 2 * margin) * width, HEAD_DIM), jnp.float32),
            pltpu.VMEM((4, KERNEL, width + 16, HEAD_DIM), jnp.float32),
            pltpu.VMEM((KERNEL, KERNEL, chans), jnp.float32),
            pltpu.VMEM((positions, planes * chans), jnp.bfloat16),
            pltpu.VMEM((8, pieces, depth, piece), jnp.bfloat16),
            pltpu.VMEM((pieces, positions, piece), jnp.float32),
            dma((4,)), dma((1,)), dma((pieces,)),
            dma((2 * heads,)), dma((2 * heads,)),
            dma((heads,)), dma((heads,)),
            dma(((planes - 1) * heads,)), dma(((planes - 1) * heads,)),
            dma((pieces,)),
            dma((pieces,)), dma((pieces,)),
            dma((pieces,)), dma((pieces,)),
            dma((pieces + 1,)), dma((pieces + 1,)),
            dma((4 * pieces,)), dma((4 * pieces,)),
        ],
        compiler_params=pltpu.CompilerParams(
            collective_id=0, has_side_effects=True, vmem_limit_bytes=VMEM_BYTES
        ),
    )(
        flat(inputs), flat(query_proj), flat(key_proj), flat(value_proj),
        depth_weight, vectors, expand_weight,
    )
    residual, hidden = pl.pallas_call(
        copy_out,
        out_shape=(
            jax.ShapeDtypeStruct((positions, chans), jnp.bfloat16),
            jax.ShapeDtypeStruct((positions, units), jnp.bfloat16),
        ),
        in_specs=[anywhere] * 2,
        out_specs=(anywhere, anywhere),
        scratch_shapes=[
            pltpu.VMEM((positions, chans), jnp.bfloat16),
            pltpu.VMEM((positions, units), jnp.bfloat16),
            dma((2 * COPY_PARTS,)),
            dma((2 * COPY_PARTS,)),
        ],
        compiler_params=pltpu.CompilerParams(vmem_limit_bytes=VMEM_BYTES),
    )(residual, hidden)
    return (residual.reshape(inputs.shape), hidden.reshape(1, rows, width, units))


def solution(mesh):
    body = on_device
    if (mesh.shape["seq"], mesh.shape["row"], mesh.shape["col"]) == (2, 4, 4):
        body = functools.partial(on_device_kernel, mesh.shape["col"])
    return jax.shard_map(
        body,
        mesh=mesh,
        in_specs=(
            P("row", "seq", None, "col"),
            P("row", "seq", None, "col"),
            P("row", "seq", None, "col"),
            P("row", "seq", None, "col"),
            P(None, None, "col"),
            P("col"),
            P(),
            P(),
            P(("seq", "row"), "col"),
            P("col"),
        ),
        out_specs=(P("row", "seq", None, "col"), P("row", "seq", None, "col")),
        check_vma=False,
    )
```
